512 devices in a mesh: ta: 8 (over z_hi, core), ha: 4 (over y), wa: 16 (over x, z_lo).
Axes of the slice: x: 4, y: 4, z: 16 (z_hi: 4, z_lo: 4; z = z_hi * 4 + z_lo), core: 2. Of those that a mesh axis runs over, the one named last changes fastest.
Arguments:
- query: bfloat16 [8, 4, 16, 64, 1792], P('ta', 'ha', 'wa'), may hold values from -80 to 80
- keys: bfloat16 [8, 4, 16, 64, 1792], P('ta', 'ha', 'wa'), may hold values from -8 to 8
- values: bfloat16 [8, 4, 16, 64, 1792], P('ta', 'ha', 'wa'), may hold values from -6 to 6
- positions: int32 [3, 8, 4, 16, 64], P(None, 'ta', 'ha', 'wa'), may hold values from 0 to 191, as said below
- window_reach: int32 [8, 4, 16, 6], P('ta', 'ha', 'wa'), may hold values 0 or 1
Outputs:
- attended: bfloat16 [8, 4, 16, 64, 1792], P('ta', 'ha', 'wa')
The draws below stay inside these ranges and needn't reach their ends.
Inputs may be any that keep to these rules, and one draw needn't show every extreme that they name: positions[1] is a common anchor plus the token's row in the slab, positions[2] is 64 plus the token's column in the slab; positions[0] is the same for all tokens of one latent frame and rises by 1 or 2 from one frame to the next.
All inputs are finite; a program needn't handle non-finite values. No bound on the sum of `window_reach` on one device may be relied on, other than what follows from the above.
Results may differ from the reference program's by a relative error of at most 0.0035.
The reference program's roundings to bfloat16 on the way (of `rot_query`, `rot_keys` and `weights`) count: a program that leaves them out, or rounds other values in their place, can miss the bound.
Values may be sent and summed in bfloat16 or wider, within the bound.
A program may use at most 64 MiB of HBM per device.

```python
import math
import jax
import jax.numpy as jnp
import numpy as np
from jax import lax

HEADS = 14
HD = 128
TILE_T = 1
TILE_H = 8
TILE_W = 8
TILE = 64
RT = 16
RH = 56
RW = 56
NTT = 8
NTH = 4
NTW = 16


def key_field(key):
    inner = jax.random.fold_in(key, 11)
    shape = (NTT, NTH, NTW, TILE, HEADS, HD)
    field = jnp.clip(jax.random.normal(inner, shape, jnp.float32), -6.0, 6.0)
    return field


def draw_keys(key, part):
    field = key_field(key)
    return field.reshape((NTT, NTH, NTW, TILE, HEADS * HD)).astype(jnp.bfloat16)


def draw_query(key, part):
    own = jax.random.fold_in(key, 3)
    shape = (NTT, NTH, NTW, TILE, HEADS, HD)
    field = jnp.clip(jax.random.normal(own, shape, jnp.float32), -6.0, 6.0)
    return field.reshape((NTT, NTH, NTW, TILE, HEADS * HD)).astype(jnp.bfloat16)


def draw_positions(key, part):
    key = jax.random.fold_in(key, 5)
    anchor = jax.random.randint(jax.random.fold_in(key, 1), (2,), 0, 64)
    frames = NTT * TILE_T
    steps_between = jax.random.randint(jax.random.fold_in(key, 2), (frames,), 1, 3)
    frame_place = jnp.cumsum(steps_between) - steps_between[0] + anchor[0]
    token = jnp.arange(TILE, dtype=jnp.int32)
    in_frame = token // (TILE_H * TILE_W)
    in_row = token // TILE_W % TILE_H
    in_col = token % TILE_W
    tile_t = jnp.arange(NTT, dtype=jnp.int32)[:, None, None, None]
    tile_h = jnp.arange(NTH, dtype=jnp.int32)[None, :, None, None]
    tile_w = jnp.arange(NTW, dtype=jnp.int32)[None, None, :, None]
    frame_index = tile_t * TILE_T + in_frame
    along_t = frame_place[frame_index] + 0 * tile_h + 0 * tile_w
    along_h = anchor[1] + tile_h * TILE_H + in_row + 0 * tile_t + 0 * tile_w
    along_w = 64 + tile_w * TILE_W + in_col + 0 * tile_t + 0 * tile_h
    return jnp.stack([along_t, along_h, along_w], axis=0).astype(jnp.int32)


def set_ends(values, rng, low, high):
    spot = [jax.random.randint(jax.random.fold_in(rng, axis), (), 0, length) for axis, length in enumerate(values.shape)]
    main_axis = values.shape.index(max(values.shape))
    next_to = spot[:main_axis] + [(spot[main_axis] + 1) % values.shape[main_axis]] + spot[main_axis + 1:]
    return values.at[tuple(spot)].set(low).at[tuple(next_to)].set(high)


def steps_of(key, shape, shards, least, high):
    level = 1.0
    for axis_at, blocks in shards:
        steps = jax.random.uniform(jax.random.fold_in(jax.random.fold_in(key, 6), axis_at), (blocks,), jnp.float32, least / len(shards), high / len(shards))
        level = level * jnp.repeat(jnp.exp(steps), shape[axis_at] // blocks).reshape((-1,) + (1,) * (len(shape) - 1 - axis_at))
    return level


def bell_draw(stream_key, extent, spread, most, cuts=(), held_as=jnp.bfloat16):
    entries = spread * jax.random.normal(stream_key, extent, jnp.float32)
    if cuts:
        entries = entries * steps_of(stream_key, extent, cuts, -0.22, 0.18)
    return jnp.clip(entries, -most, most).astype(held_as)


def setup_inputs(seed: int = 0) -> dict:
    arg_keys = jax.random.split(jax.random.key(seed), 6)
    return {
        "query": draw_query(jax.random.fold_in(arg_keys[5], 71), 0),
        "keys": draw_keys(jax.random.fold_in(arg_keys[5], 71), 0),
        "values": bell_draw(arg_keys[2], (NTT, NTH, NTW, TILE, HEADS * HD), 1.0, 6.0, ((0, 8), (1, 4), (2, 16))),
        "positions": draw_positions(jax.random.fold_in(arg_keys[5], 71), 0),
        "window_reach": set_ends((jax.random.randint(arg_keys[4], (NTT, NTH, NTW, 6), 0, 4) < 3).astype(jnp.int32), jax.random.fold_in(arg_keys[4], 1), 0, 1),
    }


def pair_freqs():
    group_sizes = [RT, RH, RW]
    table = np.zeros((3, HD // 2), np.float32)
    begin = 0
    for group in range(3):
        pairs = group_sizes[group] // 2
        local = np.arange(pairs, dtype=np.float32)
        table[group, begin:begin + pairs] = np.float32(256.0) ** (np.float32(-2.0) * local / np.float32(group_sizes[group]))
        begin += pairs
    return table

def rotate(field, positions):
    table = jnp.asarray(pair_freqs())
    place = positions.astype(jnp.float32)
    angle = place[0][..., None] * table[0] + place[1][..., None] * table[1] + place[2][..., None] * table[2]
    heads = field.shape[-1] // HD
    split = field.astype(jnp.float32).reshape(field.shape[:-1] + (heads, HD // 2, 2))
    cosine = jnp.cos(angle)[..., None, :]
    sine = jnp.sin(angle)[..., None, :]
    even = split[..., 0]
    odd = split[..., 1]
    turned = jnp.stack([even * cosine - odd * sine, even * sine + odd * cosine], axis=-1)
    return turned.reshape(field.shape).astype(jnp.bfloat16)

def reach_ok(lower, upper, place, total):
    below = (lower == 1) & (place >= 1)
    above = (upper == 1) & (place + 1 < total)
    return jnp.stack([below, jnp.ones_like(below), above], axis=-1)

def window_valid(reach, place_t, place_h, place_w, total_t, total_h, total_w):
    along_t = reach_ok(reach[..., 0], reach[..., 1], place_t, total_t)
    along_h = reach_ok(reach[..., 2], reach[..., 3], place_h, total_h)
    along_w = reach_ok(reach[..., 4], reach[..., 5], place_w, total_w)
    full = along_t[..., :, None, None] & along_h[..., None, :, None] & along_w[..., None, None, :]
    return full.reshape(full.shape[:-3] + (27,))

def reference(query, keys, values, positions, window_reach):
    rot_query = rotate(query, positions)
    rot_keys = rotate(keys, positions)
    place_t = jnp.arange(NTT, dtype=jnp.int32)[:, None, None]
    place_h = jnp.arange(NTH, dtype=jnp.int32)[None, :, None]
    place_w = jnp.arange(NTW, dtype=jnp.int32)[None, None, :]
    valid = window_valid(window_reach, place_t, place_h, place_w, NTT, NTH, NTW)
    allowed = jnp.repeat(valid, TILE, axis=-1)[..., None, :]
    scale = 1.0 / math.sqrt(HD)

    def by_head(field):
        split = field.reshape(field.shape[:-1] + (HEADS, HD))
        return jnp.moveaxis(split, -2, 0)

    def windows(field):
        padded = jnp.pad(field, ((1, 1), (1, 1), (1, 1), (0, 0), (0, 0)))
        stacked = jnp.stack([padded[a:a + NTT, b:b + NTH, c:c + NTW] for a in range(3) for b in range(3) for c in range(3)], axis=3)
        return stacked.reshape((NTT, NTH, NTW, 27 * TILE, HD))

    def one_head(operands):
        query_head, key_head, value_head = operands
        key_win = windows(key_head)
        value_win = windows(value_head)
        scores = jnp.einsum('abcqd,abckd->abcqk', query_head.astype(jnp.float32), key_win.astype(jnp.float32)) * scale
        scores = jnp.where(allowed, scores, -jnp.inf)
        largest = lax.optimization_barrier(jnp.max(scores, axis=-1, keepdims=True))
        expo = jnp.exp(scores - largest)
        total = lax.optimization_barrier(jnp.sum(expo, axis=-1, keepdims=True))
        weights = (expo / total).astype(jnp.bfloat16)
        mixed = jnp.einsum('abcqk,abckd->abcqd', weights.astype(jnp.float32), value_win.astype(jnp.float32))
        return mixed.astype(jnp.bfloat16)
    heads_out = lax.map(one_head, (by_head(rot_query), by_head(rot_keys), by_head(values)))
    return jnp.moveaxis(heads_out, 0, -2).reshape(query.shape)
```

```python
import functools
import math

import jax
import jax.numpy as jnp
import numpy as np
from jax import lax
from jax.experimental import pallas as pl
from jax.experimental.pallas import tpu as pltpu
from jax.sharding import PartitionSpec as P

HD = 128
RT = 16
RH = 56
RW = 56
GROUP = 2
NEG = -1e30
SCALE2 = math.log2(math.e) / math.sqrt(HD)
F32 = jnp.float32
BF16 = jnp.bfloat16
MESH = pl.DeviceIdType.MESH

T_UP, T_DOWN, HC_UP, HC_DOWN, HP_UP, HP_DOWN, Q_UP, Q_DOWN = range(8)
S_UP, S_DOWN, S_UP2, S_DOWN2, O_UP, O_DOWN = range(8, 14)
KINDS = 14


def freq_row():
    parts = []
    for size in (RT, RH, RW):
        pairs = size // 2
        local = np.arange(pairs, dtype=np.float32)
        parts.append(np.float32(256.0) ** (np.float32(-2.0) * local / np.float32(size)))
    return np.repeat(np.concatenate(parts), 2)[None, :].astype(np.float32)


def sin_cos(x):
    n = jnp.floor(x * F32(2.0 / math.pi) + F32(0.5))
    r = x - n * F32(1.5703125)
    r = r - n * F32(4.837512969970703125e-4)
    r = r - n * F32(7.549789954891882e-8)
    z = r * r
    s = ((F32(-1.9515295891e-4) * z + F32(8.3321608736e-3)) * z - F32(1.6666654611e-1)) * z * r + r
    c = (F32(2.443315711809948e-5) * z - F32(1.388731625493765e-3)) * z + F32(4.166664568298827e-2)
    c = c * z * z - F32(0.5) * z + F32(1.0)
    quadrant = n.astype(jnp.int32) & 3
    odd = (quadrant & 1) == 1
    sine = jnp.where(odd, c, s)
    cosine = jnp.where(odd, s, c)
    sine = jnp.where(quadrant >= 2, -sine, sine)
    cosine = jnp.where((quadrant == 1) | (quadrant == 2), -cosine, cosine)
    return sine, cosine


def kernel(
    sizes, chunks, tile,
    pos_ref, reach_ref, freq_ref, q_ref, k_ref, v_ref, out_ref,
    kv, qb, pen, bias, pbuf, st, sb, oout, oin, oacc, sincos, send_sem, recv_sem, pen_sem,
):
    nt, nh, nw = sizes
    t, h, w = lax.axis_index("ta"), lax.axis_index("ha"), lax.axis_index("wa")
    width = GROUP * HD

    def at(axis, index, size, step):
        return {axis: lax.rem(index + step + size, size)}

    t_up, t_down = at("ta", t, nt, 1), at("ta", t, nt, -1)
    h_up, h_down = at("ha", h, nh, 1), at("ha", h, nh, -1)
    w_up, w_down = at("wa", w, nw, 1), at("wa", w, nw, -1)
    w_up2, w_down2 = at("wa", w, nw, 2), at("wa", w, nw, -2)

    barrier = pltpu.get_barrier_semaphore()
    near = (t_up, t_down, h_up, h_down, w_up, w_down, w_up2, w_down2)
    for other in near:
        pl.semaphore_signal(barrier, inc=1, device_id=other, device_id_type=MESH)

    def copy(kind, c):
        src, dst, to = {
            T_UP: lambda: (kv.at[c, 0, 0], kv.at[c, 0, 1], t_up),
            T_DOWN: lambda: (kv.at[c, 0, 0], kv.at[c, 0, 2], t_down),
            HC_UP: lambda: (kv.at[c, 0, 0], kv.at[c, 1, 0], h_up),
            HC_DOWN: lambda: (kv.at[c, 0, 0], kv.at[c, 2, 0], h_down),
            HP_UP: lambda: (kv.at[c, 0, pl.ds(1, 2)], kv.at[c, 1, pl.ds(1, 2)], h_up),
            HP_DOWN: lambda: (kv.at[c, 0, pl.ds(1, 2)], kv.at[c, 2, pl.ds(1, 2)], h_down),
            Q_UP: lambda: (qb.at[c, 1], qb.at[c, 0], w_up),
            Q_DOWN: lambda: (qb.at[c, 1], qb.at[c, 2], w_down),
            S_UP: lambda: (st.at[c, 1], sb.at[c, 0], w_up),
            S_DOWN: lambda: (st.at[c, 0], sb.at[c, 1], w_down),
            S_UP2: lambda: (st.at[c, 1], sb.at[c, 2], w_up2),
            S_DOWN2: lambda: (st.at[c, 0], sb.at[c, 3], w_down2),
            O_UP: lambda: (oout.at[c, 1], oin.at[c, 0], w_up),
            O_DOWN: lambda: (oout.at[c, 0], oin.at[c, 1], w_down),
        }[kind]()
        return pltpu.make_async_remote_copy(
            src_ref=src, dst_ref=dst, send_sem=send_sem.at[c, kind], recv_sem=recv_sem.at[c, kind],
            device_id=to, device_id_type=MESH,
        )

    def pen_copy(side):
        return pltpu.make_async_remote_copy(
            src_ref=pen.at[1], dst_ref=pen.at[2 * side], send_sem=pen_sem.at[0, side],
            recv_sem=pen_sem.at[1, side], device_id=(w_up, w_down)[side], device_id_type=MESH,
        )

    row = lax.broadcasted_iota(jnp.int32, (8, HD), 0)
    closed = jnp.zeros((8, HD), F32)
    for side, edge in enumerate(
        (t >= 1, t + 1 < nt, h >= 1, h + 1 < nh, w >= 1, w + 1 < nw)
    ):
        value = jnp.where((reach_ref[0, 0, 0, side] == 1) & edge, F32(0.0), F32(NEG))
        closed = jnp.where(row == side, value, closed)
    pen[1] = closed

    dim = lax.broadcasted_iota(jnp.int32, (HD, tile), 0)
    place = [pos_ref[i, 0, 0, :, :].astype(F32) for i in range(3)]
    place = jnp.where(dim < RT, place[0], jnp.where(dim < RT + RH, place[1], place[2]))
    sine, cosine = sin_cos(place.T * freq_ref[...])
    sincos[0] = sine
    sincos[1] = cosine

    pl.semaphore_wait(barrier, len(near))
    for side in range(2):
        pen_copy(side).start()

    def rotated(ref, c, g):
        a = lax.broadcasted_iota(jnp.int32, (HD, HD), 0)
        b = lax.broadcasted_iota(jnp.int32, (HD, HD), 1)
        swap = jnp.where((a ^ 1) == b, jnp.where((b & 1) == 1, F32(1.0), F32(-1.0)), F32(0.0))
        x = ref[:, pl.ds(pl.multiple_of(c * width + g * HD, HD), HD)]
        partner = jnp.dot(x, swap.astype(BF16), preferred_element_type=F32)
        return (x.astype(F32) * sincos[1] + partner * sincos[0]).astype(BF16)

    def head(g):
        return pl.ds(g * HD, HD)

    def send_own(c, carry):
        for g in range(GROUP):
            kv[c, 0, 0, 0, :, head(g)] = rotated(k_ref, c, g)
        kv[c, 0, 0, 1] = v_ref[:, pl.ds(pl.multiple_of(c * width, HD), width)]
        copy(T_UP, c).start()
        copy(T_DOWN, c).start()
        copy(HC_UP, c).start()
        copy(HC_DOWN, c).start()
        for g in range(GROUP):
            qb[c, 1, :, head(g)] = rotated(q_ref, c, g)
        copy(Q_UP, c).start()
        copy(Q_DOWN, c).start()
        return carry

    lax.fori_loop(0, chunks, send_own, 0)

    for side in range(2):
        pen_copy(side).wait_recv()
    low = lax.broadcasted_iota(jnp.int32, (8, HD), 1) < tile
    for slot in range(3):
        rows = [jnp.broadcast_to(pen[slot, pl.ds(i, 1), :], (8, HD)) for i in range(6)]
        base = (rows[5], jnp.zeros((8, HD), F32), rows[4])[slot]
        along_t = (jnp.zeros((8, HD), F32), rows[0], rows[1])
        along_h = (jnp.zeros((8, HD), F32), rows[2], rows[3])
        tiles = [base + along_h[j] + along_t[i] for j in range(3) for i in range(3)]
        tiles.append(tiles[-1])
        for u in range(5):
            bias[slot, :, pl.ds(u * HD, HD)] = jnp.where(low, tiles[2 * u], tiles[2 * u + 1])

    keys = 9 * tile

    def relay(c):
        copy(T_UP, c).wait_recv()
        copy(T_DOWN, c).wait_recv()
        copy(HP_UP, c).start()
        copy(HP_DOWN, c).start()

    def scores(c):
        for kind in (HC_UP, HC_DOWN, HP_UP, HP_DOWN, Q_UP, Q_DOWN):
            copy(kind, c).wait_recv()
        lane = lax.broadcasted_iota(jnp.int32, (tile, HD), 1)
        stats = jnp.zeros((tile, HD), F32)
        for g in range(GROUP):
            q3 = qb[c, :, :, head(g)].reshape(3 * tile, HD)
            k9 = kv[c, :, :, 0, :, head(g)].reshape(keys, HD)
            d3 = lax.dot_general(q3, k9, (((1,), (1,)), ((), ())), preferred_element_type=F32)
            for slot in range(3):
                d = d3[slot * tile:(slot + 1) * tile] + bias[slot, pl.ds(0, 1), pl.ds(0, keys)]
                m = jnp.max(d, axis=1, keepdims=True)
                p = jnp.exp2((d - m) * F32(SCALE2))
                total = jnp.sum(p, axis=1, keepdims=True)
                pbuf[lax.rem(c, 2), g, pl.ds(slot * tile, tile), :] = p
                for base in ((0,), (4, 12), (8,))[slot]:
                    stats = jnp.where(lane == base + g, m, stats)
                    stats = jnp.where(lane == base + 2 + g, total, stats)
        turned = stats.T
        st[c, 0, :, pl.ds(0, tile)] = turned[0:8]
        st[c, 1, :, pl.ds(0, tile)] = turned[8:16]
        for kind in (S_UP, S_DOWN, S_UP2, S_DOWN2):
            copy(kind, c).start()

    def mix(c):
        for kind in (S_UP, S_DOWN, S_UP2, S_DOWN2):
            copy(kind, c).wait_recv()
        left, right = st[c, 0][:, :tile], st[c, 1][:, :tile]
        from_left, from_right = sb[c, 0][:, :tile], sb[c, 1][:, :tile]
        from_left2, from_right2 = sb[c, 2][:, :tile], sb[c, 3][:, :tile]
        factors = []
        for mine, other, third in (
            (left[0:4], from_left[4:8], from_left2[0:4]),
            (left[4:8], from_left[0:4], from_right[0:4]),
            (right[0:4], from_right[4:8], from_right2[0:4]),
        ):
            ms = [x[0:2] for x in (mine, other, third)]
            ls = [x[2:4] for x in (mine, other, third)]
            top = jnp.maximum(ms[0], jnp.maximum(ms[1], ms[2]))
            es = [jnp.exp2((m - top) * F32(SCALE2)) for m in ms]
            total = es[0] * ls[0] + es[1] * ls[1] + es[2] * ls[2]
            factors.append(es[0] / total)
        factors.append(jnp.zeros((HD - 6, tile), F32))
        factor = jnp.concatenate(factors, axis=0).T
        for g in range(GROUP):
            v9 = kv[c, :, :, 1, :, head(g)].reshape(keys, HD)
            weights = []
            for slot in range(3):
                p = pbuf[lax.rem(c, 2), g, pl.ds(slot * tile, tile), :]
                weights.append((p * factor[:, 2 * slot + g:2 * slot + g + 1]).astype(BF16))
            o3 = jnp.dot(jnp.concatenate(weights, axis=0), v9, preferred_element_type=F32)
            oout[c, 0, :, head(g)] = o3[:tile].astype(BF16)
            oout[c, 1, :, head(g)] = o3[2 * tile:].astype(BF16)
            oacc[c, :, head(g)] = o3[tile:2 * tile]
        copy(O_UP, c).start()
        copy(O_DOWN, c).start()

    def finish(c):
        copy(O_UP, c).wait_recv()
        copy(O_DOWN, c).wait_recv()
        total = oacc[c] + oin[c, 0].astype(F32) + oin[c, 1].astype(F32)
        out_ref[:, pl.ds(pl.multiple_of(c * width, HD), width)] = total.astype(BF16)

    def step(s, carry):
        for lag, stage in enumerate((relay, scores, mix, finish)):
            @pl.when((s >= lag) & (s < chunks + lag))
            def _():
                stage(s - lag)
        return carry

    lax.fori_loop(0, chunks + 3, step, 0)

    def drain(c, carry):
        for kind in range(KINDS):
            copy(kind, c).wait_send()
        return carry

    lax.fori_loop(0, chunks, drain, 0)
    for side in range(2):
        pen_copy(side).wait_send()


def body(sizes, query, keys, values, positions, window_reach):
    tile, width = query.shape[-2:]
    chunks = width // (GROUP * HD)
    wide = GROUP * HD
    vmem = pl.BlockSpec(memory_space=pltpu.VMEM)
    flat = [x.reshape(tile, width) for x in (query, keys, values)]
    out = pl.pallas_call(
        functools.partial(kernel, sizes, chunks, tile),
        out_shape=jax.ShapeDtypeStruct((tile, width), BF16),
        in_specs=[vmem, pl.BlockSpec(memory_space=pltpu.SMEM), vmem, vmem, vmem, vmem],
        out_specs=vmem,
        scratch_shapes=[
            pltpu.VMEM((chunks, 3, 3, 2, tile, wide), BF16),
            pltpu.VMEM((chunks, 3, tile, wide), BF16),
            pltpu.VMEM((3, 8, HD), F32),
            pltpu.VMEM((3, 8, 5 * HD), F32),
            pltpu.VMEM((2, GROUP, 3 * tile, 9 * tile), F32),
            pltpu.VMEM((chunks, 2, 8, HD), F32),
            pltpu.VMEM((chunks, 4, 8, HD), F32),
            pltpu.VMEM((chunks, 2, tile, wide), BF16),
            pltpu.VMEM((chunks, 2, tile, wide), BF16),
            pltpu.VMEM((chunks, tile, wide), F32),
            pltpu.VMEM((2, tile, HD), F32),
            pltpu.SemaphoreType.DMA((chunks, KINDS)),
            pltpu.SemaphoreType.DMA((chunks, KINDS)),
            pltpu.SemaphoreType.DMA((2, 2)),
        ],
        compiler_params=pltpu.CompilerParams(
            collective_id=0, has_side_effects=True, vmem_limit_bytes=40 * 1024 * 1024
        ),
        name="tile_attention",
    )(positions, window_reach, jnp.asarray(freq_row()), *flat)
    return out.reshape(query.shape)


def solution(mesh):
    in_specs = (
        P("ta", "ha", "wa", None, None),
        P("ta", "ha", "wa", None, None),
        P("ta", "ha", "wa", None, None),
        P(None, "ta", "ha", "wa", None),
        P("ta", "ha", "wa", None),
    )
    out_specs = P("ta", "ha", "wa", None, None)
    sizes = tuple(mesh.shape[a] for a in ("ta", "ha", "wa"))
    return jax.shard_map(
        functools.partial(body, sizes), mesh=mesh, in_specs=in_specs, out_specs=out_specs, check_vma=False
    )
```

```python
import functools
import math

import jax
import jax.numpy as jnp
import numpy as np
from jax import lax
from jax.experimental import pallas as pl
from jax.experimental.pallas import tpu as pltpu
from jax.sharding import PartitionSpec as P

HD = 128
RT = 16
RH = 56
RW = 56
GROUP = 2
AHEAD_K = 3
AHEAD_Q = 2
LAGS = (0, 2, 4, 6)
SLOTS = LAGS[2] - LAGS[1] + 1
NEG = -1e30
SCALE2 = math.log2(math.e) / math.sqrt(HD)
F32 = jnp.float32
BF16 = jnp.bfloat16
MESH = pl.DeviceIdType.MESH

T_UP, T_DOWN, HC_UP, HC_DOWN, HP_UP, HP_DOWN, Q_UP, Q_DOWN = range(8)
S_UP, S_DOWN, S_UP2, S_DOWN2, O_UP, O_DOWN = range(8, 14)
KINDS = 14


def freq_row():
    parts = []
    for size in (RT, RH, RW):
        pairs = size // 2
        local = np.arange(pairs, dtype=np.float32)
        parts.append(np.float32(256.0) ** (np.float32(-2.0) * local / np.float32(size)))
    return np.repeat(np.concatenate(parts), 2)[None, :].astype(np.float32)


def sin_cos(x):
    n = jnp.floor(x * F32(2.0 / math.pi) + F32(0.5))
    r = x - n * F32(1.5703125)
    r = r - n * F32(4.837512969970703125e-4)
    r = r - n * F32(7.549789954891882e-8)
    z = r * r
    s = ((F32(-1.9515295891e-4) * z + F32(8.3321608736e-3)) * z - F32(1.6666654611e-1)) * z * r + r
    c = (F32(2.443315711809948e-5) * z - F32(1.388731625493765e-3)) * z + F32(4.166664568298827e-2)
    c = c * z * z - F32(0.5) * z + F32(1.0)
    quadrant = n.astype(jnp.int32) & 3
    odd = (quadrant & 1) == 1
    sine = jnp.where(odd, c, s)
    cosine = jnp.where(odd, s, c)
    sine = jnp.where(quadrant >= 2, -sine, sine)
    cosine = jnp.where((quadrant == 1) | (quadrant == 2), -cosine, cosine)
    return sine, cosine


def kernel(
    sizes, chunks, tile,
    pos_hbm, reach_hbm, freq_hbm, q_hbm, k_hbm, v_hbm, out_ref,
    pos_ref, reach_ref, freq_ref, q_ref, k_ref, kv, qb, pen, bias, pbuf, st, sb, oout, oin, oacc, sincos, send_sem, recv_sem, pen_sem, load_sem, v_sem,
):
    nt, nh, nw = sizes
    t, h, w = lax.axis_index("ta"), lax.axis_index("ha"), lax.axis_index("wa")
    width = GROUP * HD

    t_up, t_down = {"ta": t + 1}, {"ta": t - 1}
    h_up, h_down = {"ha": h + 1}, {"ha": h - 1}
    w_up, w_down, w_up2, w_down2 = {"wa": w + 1}, {"wa": w - 1}, {"wa": w + 2}, {"wa": w - 2}
    has_t_up, has_t_down = t + 1 < nt, t >= 1
    has_h_up, has_h_down = h + 1 < nh, h >= 1
    has_w_up, has_w_down, has_w_up2, has_w_down2 = w + 1 < nw, w >= 1, w + 2 < nw, w >= 2
    near = (
        (t_up, has_t_up), (t_down, has_t_down), (h_up, has_h_up), (h_down, has_h_down),
        (w_up, has_w_up), (w_down, has_w_down), (w_up2, has_w_up2), (w_down2, has_w_down2),
    )
    upward = {T_UP, HC_UP, HP_UP, Q_UP, S_UP, S_UP2, O_UP}
    pairs = {
        T_UP: (has_t_up, has_t_down), HC_UP: (has_h_up, has_h_down), HP_UP: (has_h_up, has_h_down),
        Q_UP: (has_w_up, has_w_down), S_UP: (has_w_up, has_w_down), O_UP: (has_w_up, has_w_down),
        S_UP2: (has_w_up2, has_w_down2),
    }

    barrier = pltpu.get_barrier_semaphore()
    for other, there in near:
        @pl.when(there)
        def _():
            pl.semaphore_signal(barrier, inc=1, device_id=other, device_id_type=MESH)

    def barrier_wait():
        count = sum(there.astype(jnp.int32) for _, there in near)
        pl.semaphore_wait(barrier, count)

    loads = [
        pltpu.make_async_copy(src, dst, load_sem.at[i])
        for i, (src, dst) in enumerate(
            ((pos_hbm, pos_ref), (freq_hbm, freq_ref), (k_hbm, k_ref), (reach_hbm, reach_ref), (q_hbm, q_ref))
        )
    ]
    for load in loads:
        load.start()

    def load_v(c):
        columns = pl.ds(pl.multiple_of(c * width, HD), width)
        return pltpu.make_async_copy(v_hbm.at[:, columns], kv.at[c, 0, 0, 1], v_sem.at[c])

    for c in range(chunks):
        load_v(c).start()

    def copy(kind, c):
        src, dst, to = {
            T_UP: lambda: (kv.at[c, 0, 0], kv.at[c, 0, 1], t_up),
            T_DOWN: lambda: (kv.at[c, 0, 0], kv.at[c, 0, 2], t_down),
            HC_UP: lambda: (kv.at[c, 0, 0], kv.at[c, 1, 0], h_up),
            HC_DOWN: lambda: (kv.at[c, 0, 0], kv.at[c, 2, 0], h_down),
            HP_UP: lambda: (kv.at[c, 0, pl.ds(1, 2)], kv.at[c, 1, pl.ds(1, 2)], h_up),
            HP_DOWN: lambda: (kv.at[c, 0, pl.ds(1, 2)], kv.at[c, 2, pl.ds(1, 2)], h_down),
            Q_UP: lambda: (qb.at[c, 1], qb.at[c, 0], w_up),
            Q_DOWN: lambda: (qb.at[c, 1], qb.at[c, 2], w_down),
            S_UP: lambda: (st.at[c, 1], sb.at[c, 0], w_up),
            S_DOWN: lambda: (st.at[c, 0], sb.at[c, 1], w_down),
            S_UP2: lambda: (st.at[c, 1], sb.at[c, 2], w_up2),
            S_DOWN2: lambda: (st.at[c, 0], sb.at[c, 3], w_down2),
            O_UP: lambda: (oout.at[c, 1], oin.at[c, 0], w_up),
            O_DOWN: lambda: (oout.at[c, 0], oin.at[c, 1], w_down),
        }[kind]()
        return pltpu.make_async_remote_copy(
            src_ref=src, dst_ref=dst, send_sem=send_sem.at[c, kind], recv_sem=recv_sem.at[c, kind],
            device_id=to, device_id_type=MESH,
        )

    def guard(kind, receiving):
        up, down = pairs[kind if kind in upward else kind - 1]
        return up if (kind in upward) != receiving else down

    def start(kind, c):
        @pl.when(guard(kind, False))
        def _():
            copy(kind, c).start()

    def await_recv(kind, c):
        @pl.when(guard(kind, True))
        def _():
            copy(kind, c).wait_recv()

    def await_send(kind, c):
        @pl.when(guard(kind, False))
        def _():
            copy(kind, c).wait_send()

    def blank(c, carry):
        def fill(missing, ref, index, value=0.0):
            @pl.when(missing)
            def _():
                ref[index] = jnp.full(ref.at[index].shape, value, ref.dtype)

        fill(t < 1, kv, (c, 0, 1))
        fill(t + 1 >= nt, kv, (c, 0, 2))
        fill(h < 1, kv, (c, 1))
        fill(h + 1 >= nh, kv, (c, 2))
        for side, (one, two) in enumerate(((w < 1, w < 2), (w + 1 >= nw, w + 2 >= nw))):
            fill(one, qb, (c, 2 * side))
            fill(one, oin, (c, side))
            fill(one, pen, 2 * side)
            fill(one, sb, (c, side), NEG)
            fill(two, sb, (c, 2 + side), NEG)
        return carry

    lax.fori_loop(0, chunks, blank, 0)

    def pen_copy(side):
        return pltpu.make_async_remote_copy(
            src_ref=pen.at[1], dst_ref=pen.at[2 * side], send_sem=pen_sem.at[0, side],
            recv_sem=pen_sem.at[1, side], device_id=(w_up, w_down)[side], device_id_type=MESH,
        )

    loads[0].wait()
    loads[1].wait()
    dim = lax.broadcasted_iota(jnp.int32, (HD, tile), 0)
    place = [pos_ref[i, 0, 0, :, :].astype(F32) for i in range(3)]
    place = jnp.where(dim < RT, place[0], jnp.where(dim < RT + RH, place[1], place[2]))
    sine, cosine = sin_cos(place.T * freq_ref[...])
    sincos[0] = sine
    sincos[1] = cosine

    def rotated(ref, c, g):
        a = lax.broadcasted_iota(jnp.int32, (HD, HD), 0)
        b = lax.broadcasted_iota(jnp.int32, (HD, HD), 1)
        swap = jnp.where((a ^ 1) == b, jnp.where((b & 1) == 1, F32(1.0), F32(-1.0)), F32(0.0))
        x = ref[:, pl.ds(pl.multiple_of(c * width + g * HD, HD), HD)]
        partner = jnp.dot(x, swap.astype(BF16), preferred_element_type=F32)
        return (x.astype(F32) * sincos[1] + partner * sincos[0]).astype(BF16)

    def head(g):
        return pl.ds(g * HD, HD)

    def turn_k(c):
        for g in range(GROUP):
            kv[c, 0, 0, 0, :, head(g)] = rotated(k_ref, c, g)
        load_v(c).wait()

    def send_k(c):
        for kind in (T_UP, T_DOWN, HC_UP, HC_DOWN):
            start(kind, c)

    def send_q(c):
        for g in range(GROUP):
            qb[c, 1, :, head(g)] = rotated(q_ref, c, g)
        start(Q_UP, c)
        start(Q_DOWN, c)

    loads[2].wait()
    turn_k(0)
    barrier_wait()
    send_k(0)
    for c in range(1, min(AHEAD_K, chunks)):
        turn_k(c)
        send_k(c)

    loads[3].wait()
    row = lax.broadcasted_iota(jnp.int32, (8, HD), 0)
    closed = jnp.zeros((8, HD), F32)
    for side, edge in enumerate(
        (t >= 1, t + 1 < nt, h >= 1, h + 1 < nh, w >= 1, w + 1 < nw)
    ):
        value = jnp.where((reach_ref[0, 0, 0, side] == 1) & edge, F32(0.0), F32(NEG))
        closed = jnp.where(row == side, value, closed)
    pen[1] = closed
    for side in range(2):
        @pl.when((has_w_up, has_w_down)[side])
        def _():
            pen_copy(side).start()
    loads[4].wait()
    for c in range(min(AHEAD_Q, chunks)):
        send_q(c)

    def make_bias():
        for side in range(2):
            @pl.when((has_w_down, has_w_up)[side])
            def _():
                pen_copy(side).wait_recv()

        low = lax.broadcasted_iota(jnp.int32, (8, HD), 1) < tile
        for slot in range(3):
            rows = [jnp.broadcast_to(pen[slot, pl.ds(i, 1), :], (8, HD)) for i in range(6)]
            base = (rows[5], jnp.zeros((8, HD), F32), rows[4])[slot]
            along_t = (jnp.zeros((8, HD), F32), rows[0], rows[1])
            along_h = (jnp.zeros((8, HD), F32), rows[2], rows[3])
            tiles = [base + along_h[j] + along_t[i] for j in range(3) for i in range(3)]
            tiles.append(tiles[-1])
            for u in range(5):
                bias[slot, :, pl.ds(u * HD, HD)] = jnp.where(low, tiles[2 * u], tiles[2 * u + 1])

    keys = 9 * tile

    def relay(c):
        await_recv(T_UP, c)
        await_recv(T_DOWN, c)
        start(HP_UP, c)
        start(HP_DOWN, c)

        @pl.when(c + AHEAD_K < chunks)
        def _():
            turn_k(c + AHEAD_K)
            send_k(c + AHEAD_K)

        @pl.when(c + AHEAD_Q < chunks)
        def _():
            send_q(c + AHEAD_Q)

    def scores(c):
        @pl.when(c == 0)
        def _():
            make_bias()

        for kind in (HC_UP, HC_DOWN, HP_UP, HP_DOWN, Q_UP, Q_DOWN):
            await_recv(kind, c)
        lane = lax.broadcasted_iota(jnp.int32, (tile, HD), 1)
        stats = jnp.zeros((tile, HD), F32)
        for g in range(GROUP):
            q3 = qb[c, :, :, head(g)].reshape(3 * tile, HD)
            k9 = kv[c, :, :, 0, :, head(g)].reshape(keys, HD)
            d3 = lax.dot_general(q3, k9, (((1,), (1,)), ((), ())), preferred_element_type=F32)
            for slot in range(3):
                d = d3[slot * tile:(slot + 1) * tile] + bias[slot, pl.ds(0, 1), pl.ds(0, keys)]
                m = jnp.max(d, axis=1, keepdims=True)
                p = jnp.exp2((d - m) * F32(SCALE2))
                total = jnp.sum(p, axis=1, keepdims=True)
                pbuf[lax.rem(c, SLOTS), g, pl.ds(slot * tile, tile), :] = p
                for base in ((0,), (4, 12), (8,))[slot]:
                    stats = jnp.where(lane == base + g, m, stats)
                    stats = jnp.where(lane == base + 2 + g, total, stats)
        turned = stats.T
        st[c, 0, :, pl.ds(0, tile)] = turned[0:8]
        st[c, 1, :, pl.ds(0, tile)] = turned[8:16]
        for kind in (S_UP, S_DOWN, S_UP2, S_DOWN2):
            start(kind, c)

    def mix(c):
        for kind in (S_UP, S_DOWN, S_UP2, S_DOWN2):
            await_recv(kind, c)
        left, right = st[c, 0][:, :tile], st[c, 1][:, :tile]
        from_left, from_right = sb[c, 0][:, :tile], sb[c, 1][:, :tile]
        from_left2, from_right2 = sb[c, 2][:, :tile], sb[c, 3][:, :tile]
        factors = []
        for mine, other, third in (
            (left[0:4], from_left[4:8], from_left2[0:4]),
            (left[4:8], from_left[0:4], from_right[0:4]),
            (right[0:4], from_right[4:8], from_right2[0:4]),
        ):
            ms = [x[0:2] for x in (mine, other, third)]
            ls = [x[2:4] for x in (mine, other, third)]
            top = jnp.maximum(ms[0], jnp.maximum(ms[1], ms[2]))
            es = [jnp.exp2((m - top) * F32(SCALE2)) for m in ms]
            total = es[0] * ls[0] + es[1] * ls[1] + es[2] * ls[2]
            factors.append(es[0] / total)
        factors.append(jnp.zeros((HD - 6, tile), F32))
        factor = jnp.concatenate(factors, axis=0).T
        for g in range(GROUP):
            v9 = kv[c, :, :, 1, :, head(g)].reshape(keys, HD)
            weights = []
            for slot in range(3):
                p = pbuf[lax.rem(c, SLOTS), g, pl.ds(slot * tile, tile), :]
                weights.append((p * factor[:, 2 * slot + g:2 * slot + g + 1]).astype(BF16))
            o3 = jnp.dot(jnp.concatenate(weights, axis=0), v9, preferred_element_type=F32)
            oout[c, 0, :, head(g)] = o3[:tile].astype(BF16)
            oout[c, 1, :, head(g)] = o3[2 * tile:].astype(BF16)
            oacc[c, :, head(g)] = o3[tile:2 * tile]
        start(O_UP, c)
        start(O_DOWN, c)

    def finish(c):
        await_recv(O_UP, c)
        await_recv(O_DOWN, c)
        total = oacc[c] + oin[c, 0].astype(F32) + oin[c, 1].astype(F32)
        out_ref[:, pl.ds(pl.multiple_of(c * width, HD), width)] = total.astype(BF16)

    def step(s, carry):
        for lag, stage in zip(LAGS, (relay, scores, mix, finish)):
            @pl.when((s >= lag) & (s < chunks + lag))
            def _():
                stage(s - lag)
        return carry

    lax.fori_loop(0, chunks + LAGS[-1], step, 0)

    def drain(c, carry):
        for kind in range(KINDS):
            await_send(kind, c)
        return carry

    lax.fori_loop(0, chunks, drain, 0)
    for side in range(2):
        @pl.when((has_w_up, has_w_down)[side])
        def _():
            pen_copy(side).wait_send()


def body(sizes, query, keys, values, positions, window_reach):
    tile, width = query.shape[-2:]
    chunks = width // (GROUP * HD)
    wide = GROUP * HD
    vmem = pl.BlockSpec(memory_space=pltpu.VMEM)
    flat = [x.reshape(tile, width) for x in (query, keys, values)]
    out = pl.pallas_call(
        functools.partial(kernel, sizes, chunks, tile),
        out_shape=jax.ShapeDtypeStruct((tile, width), BF16),
        in_specs=[pl.BlockSpec(memory_space=pl.ANY)] * 6,
        out_specs=vmem,
        scratch_shapes=[
            pltpu.VMEM(positions.shape, jnp.int32),
            pltpu.SMEM(window_reach.shape, jnp.int32),
            pltpu.VMEM((1, HD), F32),
            pltpu.VMEM((tile, width), BF16),
            pltpu.VMEM((tile, width), BF16),
            pltpu.VMEM((chunks, 3, 3, 2, tile, wide), BF16),
            pltpu.VMEM((chunks, 3, tile, wide), BF16),
            pltpu.VMEM((3, 8, HD), F32),
            pltpu.VMEM((3, 8, 5 * HD), F32),
            pltpu.VMEM((SLOTS, GROUP, 3 * tile, 9 * tile), F32),
            pltpu.VMEM((chunks, 2, 8, HD), F32),
            pltpu.VMEM((chunks, 4, 8, HD), F32),
            pltpu.VMEM((chunks, 2, tile, wide), BF16),
            pltpu.VMEM((chunks, 2, tile, wide), BF16),
            pltpu.VMEM((chunks, tile, wide), F32),
            pltpu.VMEM((2, tile, HD), F32),
            pltpu.SemaphoreType.DMA((chunks, KINDS)),
            pltpu.SemaphoreType.DMA((chunks, KINDS)),
            pltpu.SemaphoreType.DMA((2, 2)),
            pltpu.SemaphoreType.DMA((5,)),
            pltpu.SemaphoreType.DMA((chunks,)),
        ],
        compiler_params=pltpu.CompilerParams(
            collective_id=0, has_side_effects=True, vmem_limit_bytes=40 * 1024 * 1024
        ),
        name="tile_attention",
    )(positions, window_reach, jnp.asarray(freq_row()), *flat)
    return out.reshape(query.shape)


def solution(mesh):
    in_specs = (
        P("ta", "ha", "wa", None, None),
        P("ta", "ha", "wa", None, None),
        P("ta", "ha", "wa", None, None),
        P(None, "ta", "ha", "wa", None),
        P("ta", "ha", "wa", None),
    )
    out_specs = P("ta", "ha", "wa", None, None)
    sizes = tuple(mesh.shape[a] for a in ("ta", "ha", "wa"))
    return jax.shard_map(
        functools.partial(body, sizes), mesh=mesh, in_specs=in_specs, out_specs=out_specs, check_vma=False
    )
```

```python
import functools
import math

import jax
import jax.numpy as jnp
import numpy as np
from jax import lax
from jax.experimental import pallas as pl
from jax.experimental.pallas import tpu as pltpu
from jax.sharding import PartitionSpec as P

HD = 128
RT = 16
RH = 56
RW = 56
GROUP = 2
AHEAD_K = 4
AHEAD_Q = 2
LAGS = (0, 2, 5, 8)
SLOTS = LAGS[2] - LAGS[1] + 1
NEG = -1e30
SCALE2 = math.log2(math.e) / math.sqrt(HD)
F32 = jnp.float32
BF16 = jnp.bfloat16
MESH = pl.DeviceIdType.MESH

T_OUT, T_IN, HC_UP, HC_DOWN, HI_UP, HI_DOWN, HO_UP, HO_DOWN, Q_UP, Q_DOWN = range(10)
S_UP, S_DOWN, S_UP2, S_DOWN2, O_UP, O_DOWN = range(10, 16)
KINDS = 16


def freq_row():
    parts = []
    for size in (RT, RH, RW):
        pairs = size // 2
        local = np.arange(pairs, dtype=np.float32)
        parts.append(np.float32(256.0) ** (np.float32(-2.0) * local / np.float32(size)))
    return np.repeat(np.concatenate(parts), 2)[None, :].astype(np.float32)


def sin_cos(x):
    n = jnp.floor(x * F32(2.0 / math.pi) + F32(0.5))
    r = x - n * F32(1.5703125)
    r = r - n * F32(4.837512969970703125e-4)
    r = r - n * F32(7.549789954891882e-8)
    z = r * r
    s = ((F32(-1.9515295891e-4) * z + F32(8.3321608736e-3)) * z - F32(1.6666654611e-1)) * z * r + r
    c = (F32(2.443315711809948e-5) * z - F32(1.388731625493765e-3)) * z + F32(4.166664568298827e-2)
    c = c * z * z - F32(0.5) * z + F32(1.0)
    quadrant = n.astype(jnp.int32) & 3
    odd = (quadrant & 1) == 1
    sine = jnp.where(odd, c, s)
    cosine = jnp.where(odd, s, c)
    sine = jnp.where(quadrant >= 2, -sine, sine)
    cosine = jnp.where((quadrant == 1) | (quadrant == 2), -cosine, cosine)
    return sine, cosine


def kernel(
    sizes, chunks, tile,
    pos_hbm, reach_hbm, freq_hbm, q_hbm, k_hbm, v_hbm, out_ref,
    pos_ref, reach_ref, freq_ref, q_ref, k_ref, kv, qb, pen, bias, pbuf, st, sb, tops, oout, oin, oacc, sincos, send_sem, recv_sem, pen_sem, load_sem, v_sem, entry_sem,
):
    nt, nh, nw = sizes
    t, h, w = lax.axis_index("ta"), lax.axis_index("ha"), lax.axis_index("wa")
    width = GROUP * HD

    odd = lax.rem(t, 2)
    even = odd == 0
    i_out, i_in = 1 + odd, 2 - odd
    t_out, t_in = {"ta": t - 1 + 2 * odd}, {"ta": t + 1 - 2 * odd}
    h_up, h_down = {"ha": h + 1}, {"ha": h - 1}
    w_up, w_down, w_up2, w_down2 = {"wa": w + 1}, {"wa": w - 1}, {"wa": w + 2}, {"wa": w - 2}
    has_out = (t - 1 + 2 * odd >= 0) & (t - 1 + 2 * odd < nt)
    always = t >= 0
    has_h_up, has_h_down = h + 1 < nh, h >= 1
    has_w_up, has_w_down, has_w_up2, has_w_down2 = w + 1 < nw, w >= 1, w + 2 < nw, w >= 2
    beside = (
        (h_up, has_h_up), (h_down, has_h_down), (w_up, has_w_up), (w_down, has_w_down),
        (w_up2, has_w_up2), (w_down2, has_w_down2),
    )
    upward = {HC_UP, HI_UP, HO_UP, Q_UP, S_UP, S_UP2, O_UP}
    pairs = {
        HC_UP: (has_h_up, has_h_down), HI_UP: (has_h_up, has_h_down),
        HO_UP: (has_h_up & has_out, has_h_down & has_out),
        Q_UP: (has_w_up, has_w_down), S_UP: (has_w_up, has_w_down), O_UP: (has_w_up, has_w_down),
        S_UP2: (has_w_up2, has_w_down2),
    }

    barrier = pltpu.get_barrier_semaphore()

    @pl.when(has_out & (odd == 1))
    def _():
        pl.semaphore_signal(barrier, inc=1, device_id=t_out, device_id_type=MESH)

    for other, there in beside:
        @pl.when(there)
        def _():
            pl.semaphore_signal(barrier, inc=1, device_id={"ta": t + 1 - odd, **other}, device_id_type=MESH)

    @pl.when(even)
    def _():
        pl.semaphore_signal(barrier, inc=1, device_id=t_in, device_id_type=MESH)

    loads = [
        pltpu.make_async_copy(src, dst, load_sem.at[i])
        for i, (src, dst) in enumerate(
            ((pos_hbm, pos_ref), (freq_hbm, freq_ref), (k_hbm, k_ref), (reach_hbm, reach_ref), (q_hbm, q_ref))
        )
    ]
    for load in loads:
        load.start()

    def load_v(c):
        columns = pl.ds(pl.multiple_of(c * width, HD), width)
        return pltpu.make_async_copy(v_hbm.at[:, columns], kv.at[c, 0, 0, 1], v_sem.at[c])

    for c in range(chunks):
        load_v(c).start()

    def copy(kind, c, landing=False):
        own, outer, inner = kv.at[c, 0, 0], kv.at[c, 0, i_out], kv.at[c, 0, i_in]
        src, dst, to = {
            T_OUT: lambda: (own, outer if landing else inner, t_out),
            T_IN: lambda: (own, inner if landing else outer, t_in),
            HC_UP: lambda: (own, kv.at[c, 1, 0], h_up),
            HC_DOWN: lambda: (own, kv.at[c, 2, 0], h_down),
            HI_UP: lambda: (inner, kv.at[c, 1, i_in], h_up),
            HI_DOWN: lambda: (inner, kv.at[c, 2, i_in], h_down),
            HO_UP: lambda: (outer, kv.at[c, 1, i_out], h_up),
            HO_DOWN: lambda: (outer, kv.at[c, 2, i_out], h_down),
            Q_UP: lambda: (qb.at[c, 1], qb.at[c, 0], w_up),
            Q_DOWN: lambda: (qb.at[c, 1], qb.at[c, 2], w_down),
            S_UP: lambda: (st.at[c, 1], sb.at[c, 0], w_up),
            S_DOWN: lambda: (st.at[c, 0], sb.at[c, 1], w_down),
            S_UP2: lambda: (st.at[c, 1, 0], sb.at[c, 2, 0], w_up2),
            S_DOWN2: lambda: (st.at[c, 0, 0], sb.at[c, 3, 0], w_down2),
            O_UP: lambda: (oout.at[c, 1], oin.at[c, 0], w_up),
            O_DOWN: lambda: (oout.at[c, 0], oin.at[c, 1], w_down),
        }[kind]()
        return pltpu.make_async_remote_copy(
            src_ref=src, dst_ref=dst, send_sem=send_sem.at[c, kind], recv_sem=recv_sem.at[c, kind],
            device_id=to, device_id_type=MESH,
        )

    def guard(kind, receiving):
        if kind in (T_OUT, T_IN):
            return has_out if kind == T_OUT else always
        up, down = pairs[kind if kind in upward else kind - 1]
        return up if (kind in upward) != receiving else down

    def start(kind, c):
        @pl.when(guard(kind, False))
        def _():
            copy(kind, c).start()

    def await_recv(kind, c):
        @pl.when(guard(kind, True))
        def _():
            copy(kind, c, True).wait_recv()

    def await_send(kind, c):
        @pl.when(guard(kind, False))
        def _():
            copy(kind, c).wait_send()

    def blank(c, carry):
        def fill(missing, ref, index, value=0.0):
            @pl.when(missing)
            def _():
                ref[index] = jnp.full(ref.at[index].shape, value, ref.dtype)

        fill(jnp.logical_not(has_out), kv, (c, slice(None), i_out))
        fill(h < 1, kv, (c, 1))
        fill(h + 1 >= nh, kv, (c, 2))
        for side, (one, two) in enumerate(((w < 1, w < 2), (w + 1 >= nw, w + 2 >= nw))):
            fill(one, qb, (c, 2 * side))
            fill(one, oin, (c, side))
            fill(one, pen, 2 * side)
            fill(one, sb, (c, side), NEG)
            fill(two, sb, (c, 2 + side), NEG)
        return carry

    lax.fori_loop(0, chunks, blank, 0)

    def pen_copy(side):
        return pltpu.make_async_remote_copy(
            src_ref=pen.at[1], dst_ref=pen.at[2 * side], send_sem=pen_sem.at[0, side],
            recv_sem=pen_sem.at[1, side], device_id=(w_up, w_down)[side], device_id_type=MESH,
        )

    loads[0].wait()
    loads[1].wait()
    dim = lax.broadcasted_iota(jnp.int32, (HD, tile), 0)
    place = [pos_ref[i, 0, 0, :, :].astype(F32) for i in range(3)]
    place = jnp.where(dim < RT, place[0], jnp.where(dim < RT + RH, place[1], place[2]))
    sine, cosine = sin_cos(place.T * freq_ref[...])
    sincos[0] = sine
    sincos[1] = cosine

    def rotated(ref, c, g):
        a = lax.broadcasted_iota(jnp.int32, (HD, HD), 0)
        b = lax.broadcasted_iota(jnp.int32, (HD, HD), 1)
        swap = jnp.where((a ^ 1) == b, jnp.where((b & 1) == 1, F32(1.0), F32(-1.0)), F32(0.0))
        x = ref[:, pl.ds(pl.multiple_of(c * width + g * HD, HD), HD)]
        partner = jnp.dot(x, swap.astype(BF16), preferred_element_type=F32)
        return (x.astype(F32) * sincos[1] + partner * sincos[0]).astype(BF16)

    def head(g):
        return pl.ds(g * HD, HD)

    def turn_k(c):
        for g in range(GROUP):
            kv[c, 0, 0, 0, :, head(g)] = rotated(k_ref, c, g)
        load_v(c).wait()

    def send_q(c):
        for g in range(GROUP):
            qb[c, 1, :, head(g)] = rotated(q_ref, c, g)
        start(Q_UP, c)
        start(Q_DOWN, c)

    loads[2].wait()
    turn_k(0)
    near_sem, out_sem = entry_sem.at[0], entry_sem.at[1]

    @pl.when(even & has_out)
    def _():
        pl.semaphore_wait(barrier, 1)
        pl.semaphore_signal(out_sem, inc=1, device_id=t_out, device_id_type=MESH)
        start(T_OUT, 0)

    for c in range(1, min(AHEAD_K, chunks)):
        turn_k(c)

        @pl.when(even & has_out)
        def _():
            start(T_OUT, c)

    @pl.when(odd == 1)
    def _():
        pl.semaphore_wait(barrier, 1 + 2 * sum(there.astype(jnp.int32) for _, there in beside))
        pl.semaphore_signal(near_sem, inc=1, device_id=t_in, device_id_type=MESH)

    @pl.when(even)
    def _():
        pl.semaphore_wait(near_sem, 1)

    loads[3].wait()
    row = lax.broadcasted_iota(jnp.int32, (8, HD), 0)
    closed = jnp.zeros((8, HD), F32)
    for side, edge in enumerate(
        (t >= 1, t + 1 < nt, h >= 1, h + 1 < nh, w >= 1, w + 1 < nw)
    ):
        value = jnp.where((reach_ref[0, 0, 0, side] == 1) & edge, F32(0.0), F32(NEG))
        closed = jnp.where(row == side, value, closed)
    pen[1] = closed
    for side in range(2):
        @pl.when((has_w_up, has_w_down)[side])
        def _():
            pen_copy(side).start()
    loads[4].wait()

    def send_own(c, carry):
        @pl.when(c >= AHEAD_K)
        def _():
            turn_k(c)

        for kind in (T_IN, HC_UP, HC_DOWN):
            start(kind, c)

        @pl.when(c < AHEAD_Q)
        def _():
            send_q(c)

        return carry

    lax.fori_loop(0, chunks, send_own, 0)

    def relay_in(c, carry):
        await_recv(T_IN, c)
        start(HI_UP, c)
        start(HI_DOWN, c)
        return carry

    lax.fori_loop(0, chunks, relay_in, 0)

    @pl.when((odd == 1) & has_out)
    def _():
        pl.semaphore_wait(out_sem, 1)
        for c in range(min(AHEAD_K, chunks)):
            start(T_OUT, c)

    def make_bias():
        for side in range(2):
            @pl.when((has_w_down, has_w_up)[side])
            def _():
                pen_copy(side).wait_recv()

        low = lax.broadcasted_iota(jnp.int32, (8, HD), 1) < tile
        for slot in range(3):
            rows = [jnp.broadcast_to(pen[slot, pl.ds(i, 1), :], (8, HD)) for i in range(6)]
            base = (rows[5], jnp.zeros((8, HD), F32), rows[4])[slot]
            along_t = (jnp.zeros((8, HD), F32), rows[0], rows[1])
            along_h = (jnp.zeros((8, HD), F32), rows[2], rows[3])
            tiles = [base + along_h[j] + along_t[i] for j in range(3) for i in range(3)]
            tiles.append(tiles[-1])
            for u in range(5):
                bias[slot, :, pl.ds(u * HD, HD)] = jnp.where(low, tiles[2 * u], tiles[2 * u + 1])

    keys = 9 * tile

    def relay(c):
        await_recv(T_OUT, c)
        start(HO_UP, c)
        start(HO_DOWN, c)

        @pl.when(c + AHEAD_K < chunks)
        def _():
            start(T_OUT, c + AHEAD_K)

        @pl.when((c + AHEAD_Q < chunks))
        def _():
            send_q(c + AHEAD_Q)

    def scores(c):
        @pl.when(c == 0)
        def _():
            make_bias()

        for kind in (HC_UP, HC_DOWN, HI_UP, HI_DOWN, HO_UP, HO_DOWN, Q_UP, Q_DOWN):
            await_recv(kind, c)
        lane = lax.broadcasted_iota(jnp.int32, (tile, HD), 1)
        stats = []
        for g in range(GROUP):
            q3 = qb[c, :, :, head(g)].reshape(3 * tile, HD)
            k9 = kv[c, :, :, 0, :, head(g)].reshape(keys, HD)
            d3 = lax.dot_general(q3, k9, (((1,), (1,)), ((), ())), preferred_element_type=F32)
            columns = jnp.zeros((tile, HD), F32)
            for slot in range(3):
                d = d3[slot * tile:(slot + 1) * tile] + bias[slot, pl.ds(0, 1), pl.ds(0, keys)]
                m = jnp.max(d, axis=1, keepdims=True)
                p = jnp.exp2((d - m) * F32(SCALE2))
                total = jnp.sum(p, axis=1, keepdims=True)
                pbuf[lax.rem(c, SLOTS), g, pl.ds(slot * tile, tile), :] = p
                columns = jnp.where(lane == slot, m * F32(SCALE2) + jnp.log2(total), columns)
                columns = jnp.where(lane == 3 + slot, m * F32(SCALE2), columns)
            stats.append(columns)
        rows = jnp.concatenate(stats, axis=0).T
        st[c, 0, 0] = rows[0:1]
        st[c, 0, 1] = rows[1:2]
        st[c, 1, 0] = rows[2:3]
        st[c, 1, 1] = rows[1:2]
        tops[lax.rem(c, SLOTS)] = rows[3:6]
        for kind in (S_UP, S_DOWN, S_UP2, S_DOWN2):
            start(kind, c)

    def mix(c):
        for kind in (S_UP, S_DOWN, S_UP2, S_DOWN2):
            await_recv(kind, c)
        mine = (st[c, 0, 0], st[c, 0, 1], st[c, 1, 0])
        near = (sb[c, 0, 1], sb[c, 0, 0], sb[c, 1, 1])
        far = (sb[c, 2, 0], sb[c, 1, 0], sb[c, 3, 0])
        mine, near, far = [jnp.concatenate(x, axis=0) for x in (mine, near, far)]
        top = jnp.maximum(mine, jnp.maximum(near, far))
        whole = top + jnp.log2(jnp.exp2(mine - top) + jnp.exp2(near - top) + jnp.exp2(far - top))
        rows = jnp.exp2(tops[lax.rem(c, SLOTS)] - whole)
        factor = jnp.concatenate([rows, jnp.zeros((HD - 3, HD), F32)], axis=0).T
        for g in range(GROUP):
            v9 = kv[c, :, :, 1, :, head(g)].reshape(keys, HD)
            weights = []
            for slot in range(3):
                p = pbuf[lax.rem(c, SLOTS), g, pl.ds(slot * tile, tile), :]
                weights.append((p * factor[g * tile:(g + 1) * tile, slot:slot + 1]).astype(BF16))
            o3 = jnp.dot(jnp.concatenate(weights, axis=0), v9, preferred_element_type=F32)
            oout[c, 0, :, head(g)] = o3[:tile].astype(BF16)
            oout[c, 1, :, head(g)] = o3[2 * tile:].astype(BF16)
            oacc[c, :, head(g)] = o3[tile:2 * tile]
        start(O_UP, c)
        start(O_DOWN, c)

    def finish(c):
        await_recv(O_UP, c)
        await_recv(O_DOWN, c)
        total = oacc[c] + oin[c, 0].astype(F32) + oin[c, 1].astype(F32)
        out_ref[:, pl.ds(pl.multiple_of(c * width, HD), width)] = total.astype(BF16)

    def step(s, carry):
        for lag, stage in zip(LAGS, (relay, scores, mix, finish)):
            @pl.when((s >= lag) & (s < chunks + lag))
            def _():
                stage(s - lag)
        return carry

    lax.fori_loop(0, chunks + LAGS[-1], step, 0)

    def drain(c, carry):
        for kind in range(KINDS):
            await_send(kind, c)
        return carry

    lax.fori_loop(0, chunks, drain, 0)
    for side in range(2):
        @pl.when((has_w_up, has_w_down)[side])
        def _():
            pen_copy(side).wait_send()


def body(sizes, query, keys, values, positions, window_reach):
    tile, width = query.shape[-2:]
    chunks = width // (GROUP * HD)
    wide = GROUP * HD
    vmem = pl.BlockSpec(memory_space=pltpu.VMEM)
    flat = [x.reshape(tile, width) for x in (query, keys, values)]
    out = pl.pallas_call(
        functools.partial(kernel, sizes, chunks, tile),
        out_shape=jax.ShapeDtypeStruct((tile, width), BF16),
        in_specs=[pl.BlockSpec(memory_space=pl.ANY)] * 6,
        out_specs=vmem,
        scratch_shapes=[
            pltpu.VMEM(positions.shape, jnp.int32),
            pltpu.SMEM(window_reach.shape, jnp.int32),
            pltpu.VMEM((1, HD), F32),
            pltpu.VMEM((tile, width), BF16),
            pltpu.VMEM((tile, width), BF16),
            pltpu.VMEM((chunks, 3, 3, 2, tile, wide), BF16),
            pltpu.VMEM((chunks, 3, tile, wide), BF16),
            pltpu.VMEM((3, 8, HD), F32),
            pltpu.VMEM((3, 8, 5 * HD), F32),
            pltpu.VMEM((SLOTS, GROUP, 3 * tile, 9 * tile), F32),
            pltpu.VMEM((chunks, 2, 2, 1, HD), F32),
            pltpu.VMEM((chunks, 4, 2, 1, HD), F32),
            pltpu.VMEM((SLOTS, 3, HD), F32),
            pltpu.VMEM((chunks, 2, tile, wide), BF16),
            pltpu.VMEM((chunks, 2, tile, wide), BF16),
            pltpu.VMEM((chunks, tile, wide), F32),
            pltpu.VMEM((2, tile, HD), F32),
            pltpu.SemaphoreType.DMA((chunks, KINDS)),
            pltpu.SemaphoreType.DMA((chunks, KINDS)),
            pltpu.SemaphoreType.DMA((2, 2)),
            pltpu.SemaphoreType.DMA((5,)),
            pltpu.SemaphoreType.DMA((chunks,)),
            pltpu.SemaphoreType.REGULAR((2,)),
        ],
        compiler_params=pltpu.CompilerParams(
            collective_id=0, has_side_effects=True, vmem_limit_bytes=40 * 1024 * 1024
        ),
        name="tile_attention",
    )(positions, window_reach, jnp.asarray(freq_row()), *flat)
    return out.reshape(query.shape)


def solution(mesh):
    in_specs = (
        P("ta", "ha", "wa", None, None),
        P("ta", "ha", "wa", None, None),
        P("ta", "ha", "wa", None, None),
        P(None, "ta", "ha", "wa", None),
        P("ta", "ha", "wa", None),
    )
    out_specs = P("ta", "ha", "wa", None, None)
    sizes = tuple(mesh.shape[a] for a in ("ta", "ha", "wa"))
    return jax.shard_map(
        functools.partial(body, sizes), mesh=mesh, in_specs=in_specs, out_specs=out_specs, check_vma=False
    )
```

```python
import functools
import math

import jax
import jax.numpy as jnp
import numpy as np
from jax import lax
from jax.experimental import pallas as pl
from jax.experimental.pallas import tpu as pltpu
from jax.sharding import PartitionSpec as P

HD = 128
RT = 16
RH = 56
RW = 56
GROUP = 2
AHEAD_K = 4
AHEAD_Q = 2
LAGS = (0, 2, 5, 8)
SLOTS = LAGS[2] - LAGS[1] + 1
NEG = -1e30
SCALE2 = math.log2(math.e) / math.sqrt(HD)
F32 = jnp.float32
BF16 = jnp.bfloat16
MESH = pl.DeviceIdType.MESH

T_OUT, T_IN, HC_UP, HC_DOWN, HI_UP, HI_DOWN, HO_UP, HO_DOWN, Q_UP, Q_DOWN = range(10)
S_UP, S_DOWN, S_UP2, S_DOWN2, O_UP, O_DOWN = range(10, 16)
KINDS = 16


def freq_row():
    parts = []
    for size in (RT, RH, RW):
        pairs = size // 2
        local = np.arange(pairs, dtype=np.float32)
        parts.append(np.float32(256.0) ** (np.float32(-2.0) * local / np.float32(size)))
    return np.repeat(np.concatenate(parts), 2)[None, :].astype(np.float32)


def sin_cos(x):
    n = jnp.floor(x * F32(2.0 / math.pi) + F32(0.5))
    r = x - n * F32(1.5703125)
    r = r - n * F32(4.837512969970703125e-4)
    r = r - n * F32(7.549789954891882e-8)
    z = r * r
    s = ((F32(-1.9515295891e-4) * z + F32(8.3321608736e-3)) * z - F32(1.6666654611e-1)) * z * r + r
    c = (F32(2.443315711809948e-5) * z - F32(1.388731625493765e-3)) * z + F32(4.166664568298827e-2)
    c = c * z * z - F32(0.5) * z + F32(1.0)
    quadrant = n.astype(jnp.int32) & 3
    odd = (quadrant & 1) == 1
    sine = jnp.where(odd, c, s)
    cosine = jnp.where(odd, s, c)
    sine = jnp.where(quadrant >= 2, -sine, sine)
    cosine = jnp.where((quadrant == 1) | (quadrant == 2), -cosine, cosine)
    return sine, cosine


def kernel(
    sizes, chunks, tile,
    pos_hbm, reach_hbm, freq_hbm, q_hbm, k_hbm, v_hbm, out_hbm,
    pos_ref, reach_ref, freq_ref, q_ref, k_ref, kv, qb, pen, bias, pbuf, st, sb, tops, oout, oin, oacc, sincos, swap_ref, out_vm, send_sem, recv_sem, pen_sem, load_sem, k_sem, v_sem, out_sem, entry_sem,
):
    nt, nh, nw = sizes
    t, h, w = lax.axis_index("ta"), lax.axis_index("ha"), lax.axis_index("wa")
    width = GROUP * HD

    odd = lax.rem(t, 2)
    even = odd == 0
    i_out, i_in = 1 + odd, 2 - odd
    t_out, t_in = {"ta": t - 1 + 2 * odd}, {"ta": t + 1 - 2 * odd}
    h_up, h_down = {"ha": h + 1}, {"ha": h - 1}
    w_up, w_down, w_up2, w_down2 = {"wa": w + 1}, {"wa": w - 1}, {"wa": w + 2}, {"wa": w - 2}
    has_out = (t - 1 + 2 * odd >= 0) & (t - 1 + 2 * odd < nt)
    always = t >= 0
    has_h_up, has_h_down = h + 1 < nh, h >= 1
    has_w_up, has_w_down, has_w_up2, has_w_down2 = w + 1 < nw, w >= 1, w + 2 < nw, w >= 2
    beside = (
        (h_up, has_h_up), (h_down, has_h_down), (w_up, has_w_up), (w_down, has_w_down),
        (w_up2, has_w_up2), (w_down2, has_w_down2),
    )
    upward = {HC_UP, HI_UP, HO_UP, Q_UP, S_UP, S_UP2, O_UP}
    pairs = {
        HC_UP: (has_h_up, has_h_down), HI_UP: (has_h_up, has_h_down),
        HO_UP: (has_h_up & has_out, has_h_down & has_out),
        Q_UP: (has_w_up, has_w_down), S_UP: (has_w_up, has_w_down), O_UP: (has_w_up, has_w_down),
        S_UP2: (has_w_up2, has_w_down2),
    }

    barrier = pltpu.get_barrier_semaphore()

    @pl.when(has_out & (odd == 1))
    def _():
        pl.semaphore_signal(barrier, inc=1, device_id=t_out, device_id_type=MESH)

    for other, there in beside:
        @pl.when(there)
        def _():
            pl.semaphore_signal(barrier, inc=1, device_id={"ta": t + 1 - odd, **other}, device_id_type=MESH)

    @pl.when(even)
    def _():
        pl.semaphore_signal(barrier, inc=1, device_id=t_in, device_id_type=MESH)

    pos_load, freq_load, reach_load, q_load = [
        pltpu.make_async_copy(src, dst, load_sem.at[i])
        for i, (src, dst) in enumerate(
            ((pos_hbm, pos_ref), (freq_hbm, freq_ref), (reach_hbm, reach_ref), (q_hbm, q_ref))
        )
    ]

    def load_k(c):
        columns = pl.ds(pl.multiple_of(c * width, HD), width)
        return pltpu.make_async_copy(k_hbm.at[:, columns], k_ref.at[:, columns], k_sem.at[c])

    def load_v(c):
        columns = pl.ds(pl.multiple_of(c * width, HD), width)
        return pltpu.make_async_copy(v_hbm.at[:, columns], kv.at[c, 0, 0, 1], v_sem.at[c])

    pos_load.start()
    freq_load.start()
    for c in range(chunks):
        load_k(c).start()
        load_v(c).start()
    reach_load.start()
    q_load.start()

    def copy(kind, c, landing=False):
        own, outer, inner = kv.at[c, 0, 0], kv.at[c, 0, i_out], kv.at[c, 0, i_in]
        src, dst, to = {
            T_OUT: lambda: (own, outer if landing else inner, t_out),
            T_IN: lambda: (own, inner if landing else outer, t_in),
            HC_UP: lambda: (own, kv.at[c, 1, 0], h_up),
            HC_DOWN: lambda: (own, kv.at[c, 2, 0], h_down),
            HI_UP: lambda: (inner, kv.at[c, 1, i_in], h_up),
            HI_DOWN: lambda: (inner, kv.at[c, 2, i_in], h_down),
            HO_UP: lambda: (outer, kv.at[c, 1, i_out], h_up),
            HO_DOWN: lambda: (outer, kv.at[c, 2, i_out], h_down),
            Q_UP: lambda: (qb.at[c, 1], qb.at[c, 0], w_up),
            Q_DOWN: lambda: (qb.at[c, 1], qb.at[c, 2], w_down),
            S_UP: lambda: (st.at[c, 1], sb.at[c, 0], w_up),
            S_DOWN: lambda: (st.at[c, 0], sb.at[c, 1], w_down),
            S_UP2: lambda: (st.at[c, 1, 0], sb.at[c, 2, 0], w_up2),
            S_DOWN2: lambda: (st.at[c, 0, 0], sb.at[c, 3, 0], w_down2),
            O_UP: lambda: (oout.at[c, 1], oin.at[c, 0], w_up),
            O_DOWN: lambda: (oout.at[c, 0], oin.at[c, 1], w_down),
        }[kind]()
        return pltpu.make_async_remote_copy(
            src_ref=src, dst_ref=dst, send_sem=send_sem.at[c, kind], recv_sem=recv_sem.at[c, kind],
            device_id=to, device_id_type=MESH,
        )

    def guard(kind, receiving):
        if kind in (T_OUT, T_IN):
            return has_out if kind == T_OUT else always
        up, down = pairs[kind if kind in upward else kind - 1]
        return up if (kind in upward) != receiving else down

    def start(kind, c):
        @pl.when(guard(kind, False))
        def _():
            copy(kind, c).start()

    def await_recv(kind, c):
        @pl.when(guard(kind, True))
        def _():
            copy(kind, c, True).wait_recv()

    def await_send(kind, c):
        @pl.when(guard(kind, False))
        def _():
            copy(kind, c).wait_send()

    def blank(c, carry):
        def fill(missing, ref, index, value=0.0):
            @pl.when(missing)
            def _():
                ref[index] = jnp.full(ref.at[index].shape, value, ref.dtype)

        fill(jnp.logical_not(has_out), kv, (c, slice(None), i_out))
        fill(h < 1, kv, (c, 1))
        fill(h + 1 >= nh, kv, (c, 2))
        for side, (one, two) in enumerate(((w < 1, w < 2), (w + 1 >= nw, w + 2 >= nw))):
            fill(one, qb, (c, 2 * side))
            fill(one, oin, (c, side))
            fill(one, pen, 2 * side)
            fill(one, sb, (c, side), NEG)
            fill(two, sb, (c, 2 + side), NEG)
        return carry

    def pen_copy(side):
        return pltpu.make_async_remote_copy(
            src_ref=pen.at[1], dst_ref=pen.at[2 * side], send_sem=pen_sem.at[0, side],
            recv_sem=pen_sem.at[1, side], device_id=(w_up, w_down)[side], device_id_type=MESH,
        )

    a = lax.broadcasted_iota(jnp.int32, (HD, HD), 0)
    b = lax.broadcasted_iota(jnp.int32, (HD, HD), 1)
    swap = jnp.where((a ^ 1) == b, jnp.where((b & 1) == 1, F32(1.0), F32(-1.0)), F32(0.0))
    swap_ref[...] = swap.astype(BF16)
    pos_load.wait()
    freq_load.wait()
    dim = lax.broadcasted_iota(jnp.int32, (HD, tile), 0)
    place = [pos_ref[i, 0, 0, :, :].astype(F32) for i in range(3)]
    place = jnp.where(dim < RT, place[0], jnp.where(dim < RT + RH, place[1], place[2]))
    sine, cosine = sin_cos(place.T * freq_ref[...])
    sincos[0] = sine
    sincos[1] = cosine

    def rotated(ref, c, g):
        x = ref[:, pl.ds(pl.multiple_of(c * width + g * HD, HD), HD)]
        partner = jnp.dot(x, swap_ref[...], preferred_element_type=F32)
        return (x.astype(F32) * sincos[1] + partner * sincos[0]).astype(BF16)

    def head(g):
        return pl.ds(g * HD, HD)

    def turn_k(c):
        load_k(c).wait()
        for g in range(GROUP):
            kv[c, 0, 0, 0, :, head(g)] = rotated(k_ref, c, g)
        load_v(c).wait()

    def send_q(c):
        for g in range(GROUP):
            qb[c, 1, :, head(g)] = rotated(q_ref, c, g)
        start(Q_UP, c)
        start(Q_DOWN, c)

    turn_k(0)
    near_sem, far_sem = entry_sem.at[0], entry_sem.at[1]

    @pl.when(even & has_out)
    def _():
        pl.semaphore_wait(barrier, 1)
        pl.semaphore_signal(far_sem, inc=1, device_id=t_out, device_id_type=MESH)
        start(T_OUT, 0)

    for c in range(1, min(AHEAD_K, chunks)):
        turn_k(c)

        @pl.when(even & has_out)
        def _():
            start(T_OUT, c)

    @pl.when(odd == 1)
    def _():
        pl.semaphore_wait(barrier, 1 + 2 * sum(there.astype(jnp.int32) for _, there in beside))
        pl.semaphore_signal(near_sem, inc=1, device_id=t_in, device_id_type=MESH)

    @pl.when(even)
    def _():
        pl.semaphore_wait(near_sem, 1)

    lax.fori_loop(0, chunks, blank, 0)

    reach_load.wait()
    row = lax.broadcasted_iota(jnp.int32, (8, HD), 0)
    closed = jnp.zeros((8, HD), F32)
    for side, edge in enumerate(
        (t >= 1, t + 1 < nt, h >= 1, h + 1 < nh, w >= 1, w + 1 < nw)
    ):
        value = jnp.where((reach_ref[0, 0, 0, side] == 1) & edge, F32(0.0), F32(NEG))
        closed = jnp.where(row == side, value, closed)
    pen[1] = closed
    for side in range(2):
        @pl.when((has_w_up, has_w_down)[side])
        def _():
            pen_copy(side).start()
    q_load.wait()

    def send_own(c, carry):
        @pl.when(c >= AHEAD_K)
        def _():
            turn_k(c)

        for kind in (T_IN, HC_UP, HC_DOWN):
            start(kind, c)

        @pl.when(c < AHEAD_Q)
        def _():
            send_q(c)

        return carry

    lax.fori_loop(0, chunks, send_own, 0)

    def relay_in(c, carry):
        await_recv(T_IN, c)
        start(HI_UP, c)
        start(HI_DOWN, c)
        return carry

    lax.fori_loop(0, chunks, relay_in, 0)

    @pl.when((odd == 1) & has_out)
    def _():
        pl.semaphore_wait(far_sem, 1)
        for c in range(min(AHEAD_K, chunks)):
            start(T_OUT, c)

    def make_bias():
        for side in range(2):
            @pl.when((has_w_down, has_w_up)[side])
            def _():
                pen_copy(side).wait_recv()

        low = lax.broadcasted_iota(jnp.int32, (8, HD), 1) < tile
        for slot in range(3):
            rows = [jnp.broadcast_to(pen[slot, pl.ds(i, 1), :], (8, HD)) for i in range(6)]
            base = (rows[5], jnp.zeros((8, HD), F32), rows[4])[slot]
            along_t = (jnp.zeros((8, HD), F32), rows[0], rows[1])
            along_h = (jnp.zeros((8, HD), F32), rows[2], rows[3])
            tiles = [base + along_h[j] + along_t[i] for j in range(3) for i in range(3)]
            tiles.append(tiles[-1])
            for u in range(5):
                bias[slot, :, pl.ds(u * HD, HD)] = jnp.where(low, tiles[2 * u], tiles[2 * u + 1])

    keys = 9 * tile

    def relay(c):
        await_recv(T_OUT, c)
        start(HO_UP, c)
        start(HO_DOWN, c)

        @pl.when(c + AHEAD_K < chunks)
        def _():
            start(T_OUT, c + AHEAD_K)

        @pl.when(c + AHEAD_Q < chunks)
        def _():
            send_q(c + AHEAD_Q)

    def scores(c):
        @pl.when(c == 0)
        def _():
            make_bias()

        for kind in (HC_UP, HC_DOWN, HI_UP, HI_DOWN, HO_UP, HO_DOWN, Q_UP, Q_DOWN):
            await_recv(kind, c)
        lane = lax.broadcasted_iota(jnp.int32, (tile, HD), 1)
        stats = []
        for g in range(GROUP):
            q3 = qb[c, :, :, head(g)].reshape(3 * tile, HD)
            k9 = kv[c, :, :, 0, :, head(g)].reshape(keys, HD)
            d3 = lax.dot_general(q3, k9, (((1,), (1,)), ((), ())), preferred_element_type=F32)
            columns = jnp.zeros((tile, HD), F32)
            for slot in range(3):
                d = d3[slot * tile:(slot + 1) * tile] + bias[slot, pl.ds(0, 1), pl.ds(0, keys)]
                m = jnp.max(d, axis=1, keepdims=True)
                p = jnp.exp2((d - m) * F32(SCALE2))
                total = jnp.sum(p, axis=1, keepdims=True)
                pbuf[lax.rem(c, SLOTS), g, pl.ds(slot * tile, tile), :] = p
                columns = jnp.where(lane == slot, m * F32(SCALE2) + jnp.log2(total), columns)
                columns = jnp.where(lane == 3 + slot, m * F32(SCALE2), columns)
            stats.append(columns)
        rows = jnp.concatenate(stats, axis=0).T
        st[c, 0, 0] = rows[0:1]
        st[c, 0, 1] = rows[1:2]
        st[c, 1, 0] = rows[2:3]
        st[c, 1, 1] = rows[1:2]
        tops[lax.rem(c, SLOTS)] = rows[3:6]
        for kind in (S_UP, S_DOWN, S_UP2, S_DOWN2):
            start(kind, c)

    def mix(c):
        for kind in (S_UP, S_DOWN, S_UP2, S_DOWN2):
            await_recv(kind, c)
        mine = (st[c, 0, 0], st[c, 0, 1], st[c, 1, 0])
        near = (sb[c, 0, 1], sb[c, 0, 0], sb[c, 1, 1])
        far = (sb[c, 2, 0], sb[c, 1, 0], sb[c, 3, 0])
        mine, near, far = [jnp.concatenate(x, axis=0) for x in (mine, near, far)]
        top = jnp.maximum(mine, jnp.maximum(near, far))
        whole = top + jnp.log2(jnp.exp2(mine - top) + jnp.exp2(near - top) + jnp.exp2(far - top))
        rows = jnp.exp2(tops[lax.rem(c, SLOTS)] - whole)
        factor = jnp.concatenate([rows, jnp.zeros((HD - 3, HD), F32)], axis=0).T
        for g in range(GROUP):
            v9 = kv[c, :, :, 1, :, head(g)].reshape(keys, HD)
            weights = []
            for slot in range(3):
                p = pbuf[lax.rem(c, SLOTS), g, pl.ds(slot * tile, tile), :]
                weights.append((p * factor[g * tile:(g + 1) * tile, slot:slot + 1]).astype(BF16))
            o3 = jnp.dot(jnp.concatenate(weights, axis=0), v9, preferred_element_type=F32)
            oout[c, 0, :, head(g)] = o3[:tile].astype(BF16)
            oout[c, 1, :, head(g)] = o3[2 * tile:].astype(BF16)
            oacc[c, :, head(g)] = o3[tile:2 * tile]
        start(O_UP, c)
        start(O_DOWN, c)

    def store(c):
        columns = pl.ds(pl.multiple_of(c * width, HD), width)
        return pltpu.make_async_copy(out_vm.at[:, columns], out_hbm.at[:, columns], out_sem.at[c])

    def settle(c):
        await_send(O_UP, c)
        await_send(O_DOWN, c)
        store(c).wait()

    def finish(c):
        await_recv(O_UP, c)
        await_recv(O_DOWN, c)
        total = oacc[c] + oin[c, 0].astype(F32) + oin[c, 1].astype(F32)
        out_vm[:, pl.ds(pl.multiple_of(c * width, HD), width)] = total.astype(BF16)
        store(c).start()
        for kind in range(O_UP):
            await_send(kind, c)

        @pl.when(c >= 1)
        def _():
            settle(c - 1)


    def step(s, carry):
        for lag, stage in zip(LAGS, (relay, scores, mix, finish)):
            @pl.when((s >= lag) & (s < chunks + lag))
            def _():
                stage(s - lag)
        return carry

    lax.fori_loop(0, chunks + LAGS[-1], step, 0)

    settle(chunks - 1)
    for side in range(2):
        @pl.when((has_w_up, has_w_down)[side])
        def _():
            pen_copy(side).wait_send()


def body(sizes, query, keys, values, positions, window_reach):
    tile, width = query.shape[-2:]
    chunks = width // (GROUP * HD)
    wide = GROUP * HD
    flat = [x.reshape(tile, width) for x in (query, keys, values)]
    out = pl.pallas_call(
        functools.partial(kernel, sizes, chunks, tile),
        out_shape=jax.ShapeDtypeStruct((tile, width), BF16),
        in_specs=[pl.BlockSpec(memory_space=pltpu.HBM)] * 6,
        out_specs=pl.BlockSpec(memory_space=pltpu.HBM),
        scratch_shapes=[
            pltpu.VMEM(positions.shape, jnp.int32),
            pltpu.SMEM(window_reach.shape, jnp.int32),
            pltpu.VMEM((1, HD), F32),
            pltpu.VMEM((tile, width), BF16),
            pltpu.VMEM((tile, width), BF16),
            pltpu.VMEM((chunks, 3, 3, 2, tile, wide), BF16),
            pltpu.VMEM((chunks, 3, tile, wide), BF16),
            pltpu.VMEM((3, 8, HD), F32),
            pltpu.VMEM((3, 8, 5 * HD), F32),
            pltpu.VMEM((SLOTS, GROUP, 3 * tile, 9 * tile), F32),
            pltpu.VMEM((chunks, 2, 2, 1, HD), F32),
            pltpu.VMEM((chunks, 4, 2, 1, HD), F32),
            pltpu.VMEM((SLOTS, 3, HD), F32),
            pltpu.VMEM((chunks, 2, tile, wide), BF16),
            pltpu.VMEM((chunks, 2, tile, wide), BF16),
            pltpu.VMEM((chunks, tile, wide), F32),
            pltpu.VMEM((2, tile, HD), F32),
            pltpu.VMEM((HD, HD), BF16),
            pltpu.VMEM((tile, width), BF16),
            pltpu.SemaphoreType.DMA((chunks, KINDS)),
            pltpu.SemaphoreType.DMA((chunks, KINDS)),
            pltpu.SemaphoreType.DMA((2, 2)),
            pltpu.SemaphoreType.DMA((4,)),
            pltpu.SemaphoreType.DMA((chunks,)),
            pltpu.SemaphoreType.DMA((chunks,)),
            pltpu.SemaphoreType.DMA((chunks,)),
            pltpu.SemaphoreType.REGULAR((2,)),
        ],
        compiler_params=pltpu.CompilerParams(
            collective_id=0, has_side_effects=True, vmem_limit_bytes=64 * 1024 * 1024
        ),
        name="tile_attention",
    )(positions, window_reach, jnp.asarray(freq_row()), *flat)
    return out.reshape(query.shape)


def solution(mesh):
    in_specs = (
        P("ta", "ha", "wa", None, None),
        P("ta", "ha", "wa", None, None),
        P("ta", "ha", "wa", None, None),
        P(None, "ta", "ha", "wa", None),
        P("ta", "ha", "wa", None),
    )
    out_specs = P("ta", "ha", "wa", None, None)
    sizes = tuple(mesh.shape[a] for a in ("ta", "ha", "wa"))
    return jax.shard_map(
        functools.partial(body, sizes), mesh=mesh, in_specs=in_specs, out_specs=out_specs, check_vma=False
    )
```

```python
import functools
import math

import jax
import jax.numpy as jnp
import numpy as np
from jax import lax
from jax.experimental import pallas as pl
from jax.experimental.pallas import tpu as pltpu
from jax.sharding import PartitionSpec as P

HD = 128
RT = 16
RH = 56
RW = 56
GROUP = 2
AHEAD_K = 4
AHEAD_Q = 2
LAGS = (0, 2, 5, 8)
SLOTS = LAGS[2] - LAGS[1] + 1
NEG = -1e30
SCALE2 = math.log2(math.e) / math.sqrt(HD)
F32 = jnp.float32
BF16 = jnp.bfloat16
MESH = pl.DeviceIdType.MESH

T_OUT, T_IN, HC_UP, HC_DOWN, HI_UP, HI_DOWN, HO_UP, HO_DOWN, Q_UP, Q_DOWN = range(10)
S_UP, S_DOWN, S_UP2, S_DOWN2, O_UP, O_DOWN = range(10, 16)
KINDS = 16


def freq_row():
    parts = []
    for size in (RT, RH, RW):
        pairs = size // 2
        local = np.arange(pairs, dtype=np.float32)
        parts.append(np.float32(256.0) ** (np.float32(-2.0) * local / np.float32(size)))
    return np.repeat(np.concatenate(parts), 2)[None, :].astype(np.float32)


def sin_cos(x):
    n = jnp.floor(x * F32(2.0 / math.pi) + F32(0.5))
    r = x - n * F32(1.5703125)
    r = r - n * F32(4.837512969970703125e-4)
    r = r - n * F32(7.549789954891882e-8)
    z = r * r
    s = ((F32(-1.9515295891e-4) * z + F32(8.3321608736e-3)) * z - F32(1.6666654611e-1)) * z * r + r
    c = (F32(2.443315711809948e-5) * z - F32(1.388731625493765e-3)) * z + F32(4.166664568298827e-2)
    c = c * z * z - F32(0.5) * z + F32(1.0)
    quadrant = n.astype(jnp.int32) & 3
    odd = (quadrant & 1) == 1
    sine = jnp.where(odd, c, s)
    cosine = jnp.where(odd, s, c)
    sine = jnp.where(quadrant >= 2, -sine, sine)
    cosine = jnp.where((quadrant == 1) | (quadrant == 2), -cosine, cosine)
    return sine, cosine


def kernel(
    sizes, chunks, tile,
    pos_hbm, reach_hbm, freq_hbm, q_hbm, k_hbm, v_hbm, out_hbm,
    pos_ref, reach_ref, freq_ref, q_ref, k_ref, kv, qb, pen, bias, pbuf, st, sb, tops, oout, oin, oacc, sincos, swap_ref, out_vm, send_sem, recv_sem, pen_sem, load_sem, k_sem, v_sem, out_sem, entry_sem,
):
    nt, nh, nw = sizes
    t, h, w = lax.axis_index("ta"), lax.axis_index("ha"), lax.axis_index("wa")
    width = GROUP * HD

    odd = lax.rem(t, 2)
    even = odd == 0
    i_out, i_in = 1 + odd, 2 - odd
    t_out, t_in = {"ta": t - 1 + 2 * odd}, {"ta": t + 1 - 2 * odd}
    h_up, h_down = {"ha": h + 1}, {"ha": h - 1}
    w_up, w_down, w_up2, w_down2 = {"wa": w + 1}, {"wa": w - 1}, {"wa": w + 2}, {"wa": w - 2}
    has_out = (t - 1 + 2 * odd >= 0) & (t - 1 + 2 * odd < nt)
    always = t >= 0
    has_h_up, has_h_down = h + 1 < nh, h >= 1
    has_w_up, has_w_down, has_w_up2, has_w_down2 = w + 1 < nw, w >= 1, w + 2 < nw, w >= 2
    beside = (
        (h_up, has_h_up), (h_down, has_h_down), (w_up, has_w_up), (w_down, has_w_down),
        (w_up2, has_w_up2), (w_down2, has_w_down2),
    )
    upward = {HC_UP, HI_UP, HO_UP, Q_UP, S_UP, S_UP2, O_UP}
    pairs = {
        HC_UP: (has_h_up, has_h_down), HI_UP: (has_h_up, has_h_down),
        HO_UP: (has_h_up & has_out, has_h_down & has_out),
        Q_UP: (has_w_up, has_w_down), S_UP: (has_w_up, has_w_down), O_UP: (has_w_up, has_w_down),
        S_UP2: (has_w_up2, has_w_down2),
    }

    barrier = pltpu.get_barrier_semaphore()

    @pl.when(has_out & (odd == 1))
    def _():
        pl.semaphore_signal(barrier, inc=1, device_id=t_out, device_id_type=MESH)

    for other, there in beside:
        @pl.when(there)
        def _():
            pl.semaphore_signal(barrier, inc=1, device_id={"ta": t + 1 - odd, **other}, device_id_type=MESH)

    @pl.when(even)
    def _():
        pl.semaphore_signal(barrier, inc=1, device_id=t_in, device_id_type=MESH)

    pos_load, freq_load, reach_load, q_load = [
        pltpu.make_async_copy(src, dst, load_sem.at[i])
        for i, (src, dst) in enumerate(
            ((pos_hbm, pos_ref), (freq_hbm, freq_ref), (reach_hbm, reach_ref), (q_hbm, q_ref))
        )
    ]

    def load_k(c):
        columns = pl.ds(pl.multiple_of(c * width, HD), width)
        return pltpu.make_async_copy(k_hbm.at[:, columns], k_ref.at[:, columns], k_sem.at[c])

    def load_v(c):
        columns = pl.ds(pl.multiple_of(c * width, HD), width)
        return pltpu.make_async_copy(v_hbm.at[:, columns], kv.at[c, 0, 0, 1], v_sem.at[c])

    pos_load.start()
    freq_load.start()
    for c in range(chunks):
        load_k(c).start()
        load_v(c).start()
    reach_load.start()
    q_load.start()

    def copy(kind, c, landing=False):
        own, outer, inner = kv.at[c, 0, 0], kv.at[c, 0, i_out], kv.at[c, 0, i_in]
        src, dst, to = {
            T_OUT: lambda: (own, outer if landing else inner, t_out),
            T_IN: lambda: (own, inner if landing else outer, t_in),
            HC_UP: lambda: (own, kv.at[c, 1, 0], h_up),
            HC_DOWN: lambda: (own, kv.at[c, 2, 0], h_down),
            HI_UP: lambda: (inner, kv.at[c, 1, i_in], h_up),
            HI_DOWN: lambda: (inner, kv.at[c, 2, i_in], h_down),
            HO_UP: lambda: (outer, kv.at[c, 1, i_out], h_up),
            HO_DOWN: lambda: (outer, kv.at[c, 2, i_out], h_down),
            Q_UP: lambda: (qb.at[c, 1], qb.at[c, 0], w_up),
            Q_DOWN: lambda: (qb.at[c, 1], qb.at[c, 2], w_down),
            S_UP: lambda: (st.at[c, 1], sb.at[c, 0], w_up),
            S_DOWN: lambda: (st.at[c, 0], sb.at[c, 1], w_down),
            S_UP2: lambda: (st.at[c, 1, 0], sb.at[c, 2, 0], w_up2),
            S_DOWN2: lambda: (st.at[c, 0, 0], sb.at[c, 3, 0], w_down2),
            O_UP: lambda: (oout.at[c, 1], oin.at[c, 0], w_up),
            O_DOWN: lambda: (oout.at[c, 0], oin.at[c, 1], w_down),
        }[kind]()
        return pltpu.make_async_remote_copy(
            src_ref=src, dst_ref=dst, send_sem=send_sem.at[c, kind], recv_sem=recv_sem.at[c, kind],
            device_id=to, device_id_type=MESH,
        )

    def guard(kind, receiving):
        if kind in (T_OUT, T_IN):
            return has_out if kind == T_OUT else always
        up, down = pairs[kind if kind in upward else kind - 1]
        return up if (kind in upward) != receiving else down

    def start(kind, c):
        @pl.when(guard(kind, False))
        def _():
            copy(kind, c).start()

    def await_recv(kind, c):
        @pl.when(guard(kind, True))
        def _():
            copy(kind, c, True).wait_recv()

    def await_send(kind, c):
        @pl.when(guard(kind, False))
        def _():
            copy(kind, c).wait_send()

    def blank(c, carry):
        def fill(missing, ref, index, value=0.0):
            @pl.when(missing)
            def _():
                ref[index] = jnp.full(ref.at[index].shape, value, ref.dtype)

        fill(jnp.logical_not(has_out), kv, (c, slice(None), i_out))
        fill(h < 1, kv, (c, 1))
        fill(h + 1 >= nh, kv, (c, 2))
        for side, (one, two) in enumerate(((w < 1, w < 2), (w + 1 >= nw, w + 2 >= nw))):
            fill(one, qb, (c, 2 * side))
            fill(one, oin, (c, side))
            fill(one, pen, 2 * side)
            fill(one, sb, (c, side), NEG)
            fill(two, sb, (c, 2 + side), NEG)
        return carry

    def pen_copy(side):
        return pltpu.make_async_remote_copy(
            src_ref=pen.at[1], dst_ref=pen.at[2 * side], send_sem=pen_sem.at[0, side],
            recv_sem=pen_sem.at[1, side], device_id=(w_up, w_down)[side], device_id_type=MESH,
        )

    a = lax.broadcasted_iota(jnp.int32, (HD, HD), 0)
    b = lax.broadcasted_iota(jnp.int32, (HD, HD), 1)
    swap = jnp.where((a ^ 1) == b, jnp.where((b & 1) == 1, F32(1.0), F32(-1.0)), F32(0.0))
    swap_ref[...] = swap.astype(BF16)
    pos_load.wait()
    freq_load.wait()
    dim = lax.broadcasted_iota(jnp.int32, (HD, tile), 0)
    place = [pos_ref[i, 0, 0, :, :].astype(F32) for i in range(3)]
    place = jnp.where(dim < RT, place[0], jnp.where(dim < RT + RH, place[1], place[2]))
    sine, cosine = sin_cos(place.T * freq_ref[...])
    sincos[0] = sine
    sincos[1] = cosine

    def rotated(ref, c, g):
        x = ref[:, pl.ds(pl.multiple_of(c * width + g * HD, HD), HD)]
        partner = jnp.dot(x, swap_ref[...], preferred_element_type=F32)
        return (x.astype(F32) * sincos[1] + partner * sincos[0]).astype(BF16)

    def head(g):
        return pl.ds(g * HD, HD)

    def turn_k(c):
        load_k(c).wait()
        for g in range(GROUP):
            kv[c, 0, 0, 0, :, head(g)] = rotated(k_ref, c, g)
        load_v(c).wait()

    def send_q(c):
        for g in range(GROUP):
            qb[c, 1, :, head(g)] = rotated(q_ref, c, g)
        start(Q_UP, c)
        start(Q_DOWN, c)

    turn_k(0)
    near_sem, far_sem = entry_sem.at[0], entry_sem.at[1]

    @pl.when(even & has_out)
    def _():
        pl.semaphore_wait(barrier, 1)
        pl.semaphore_signal(far_sem, inc=1, device_id=t_out, device_id_type=MESH)
        start(T_OUT, 0)

    for c in range(1, min(AHEAD_K, chunks)):
        turn_k(c)

        @pl.when(even & has_out)
        def _():
            start(T_OUT, c)

    @pl.when(odd == 1)
    def _():
        pl.semaphore_wait(barrier, 1 + 2 * sum(there.astype(jnp.int32) for _, there in beside))
        pl.semaphore_signal(near_sem, inc=1, device_id=t_in, device_id_type=MESH)

    @pl.when(even)
    def _():
        pl.semaphore_wait(near_sem, 1)

    lax.fori_loop(0, chunks, blank, 0)

    reach_load.wait()
    row = lax.broadcasted_iota(jnp.int32, (8, HD), 0)
    closed = jnp.zeros((8, HD), F32)
    for side, edge in enumerate(
        (t >= 1, t + 1 < nt, h >= 1, h + 1 < nh, w >= 1, w + 1 < nw)
    ):
        value = jnp.where((reach_ref[0, 0, 0, side] == 1) & edge, F32(0.0), F32(NEG))
        closed = jnp.where(row == side, value, closed)
    pen[1] = closed
    for side in range(2):
        @pl.when((has_w_up, has_w_down)[side])
        def _():
            pen_copy(side).start()
    q_load.wait()

    def send_own(c, carry):
        @pl.when(c >= AHEAD_K)
        def _():
            turn_k(c)

        for kind in (T_IN, HC_UP, HC_DOWN):
            start(kind, c)

        @pl.when(c < AHEAD_Q)
        def _():
            send_q(c)

        return carry

    lax.fori_loop(0, chunks, send_own, 0)

    def relay_in(c, carry):
        await_recv(T_IN, c)
        start(HI_UP, c)
        start(HI_DOWN, c)
        return carry

    lax.fori_loop(0, chunks, relay_in, 0)

    @pl.when((odd == 1) & has_out)
    def _():
        pl.semaphore_wait(far_sem, 1)
        for c in range(min(AHEAD_K, chunks)):
            start(T_OUT, c)

    def make_bias():
        for side in range(2):
            @pl.when((has_w_down, has_w_up)[side])
            def _():
                pen_copy(side).wait_recv()

        low = lax.broadcasted_iota(jnp.int32, (8, HD), 1) < tile
        for slot in range(3):
            rows = [jnp.broadcast_to(pen[slot, pl.ds(i, 1), :], (8, HD)) for i in range(6)]
            base = (rows[5], jnp.zeros((8, HD), F32), rows[4])[slot]
            along_t = (jnp.zeros((8, HD), F32), rows[0], rows[1])
            along_h = (jnp.zeros((8, HD), F32), rows[2], rows[3])
            tiles = [base + along_h[j] + along_t[i] for j in range(3) for i in range(3)]
            tiles.append(tiles[-1])
            for u in range(5):
                bias[slot, :, pl.ds(u * HD, HD)] = jnp.where(low, tiles[2 * u], tiles[2 * u + 1])

    keys = 9 * tile

    def relay(c):
        await_recv(T_OUT, c)
        start(HO_UP, c)
        start(HO_DOWN, c)

        @pl.when(c + AHEAD_K < chunks)
        def _():
            start(T_OUT, c + AHEAD_K)

        @pl.when(c + AHEAD_Q < chunks)
        def _():
            send_q(c + AHEAD_Q)

    def scores(c):
        @pl.when(c == 0)
        def _():
            make_bias()

        for kind in (HC_UP, HC_DOWN, HI_UP, HI_DOWN, HO_UP, HO_DOWN, Q_UP, Q_DOWN):
            await_recv(kind, c)
        lane = lax.broadcasted_iota(jnp.int32, (tile, HD), 1)
        stats = []
        for g in range(GROUP):
            q3 = qb[c, :, :, head(g)].reshape(3 * tile, HD)
            k9 = kv[c, :, :, 0, :, head(g)].reshape(keys, HD)
            d3 = lax.dot_general(q3, k9, (((1,), (1,)), ((), ())), preferred_element_type=F32)
            columns = jnp.zeros((tile, HD), F32)
            for slot in range(3):
                d = d3[slot * tile:(slot + 1) * tile] + bias[slot, pl.ds(0, 1), pl.ds(0, keys)]
                m = jnp.max(d, axis=1, keepdims=True)
                p = jnp.exp2((d - m) * F32(SCALE2))
                total = jnp.sum(p, axis=1, keepdims=True)
                pbuf[lax.rem(c, SLOTS), g, pl.ds(slot * tile, tile), :] = p
                columns = jnp.where(lane == slot, m * F32(SCALE2) + jnp.log2(total), columns)
                columns = jnp.where(lane == 3 + slot, m * F32(SCALE2), columns)
            stats.append(columns)
        rows = jnp.concatenate(stats, axis=0).T
        st[c, 0, 0] = rows[0:1]
        st[c, 0, 1] = rows[1:2]
        st[c, 1, 0] = rows[2:3]
        st[c, 1, 1] = rows[1:2]
        tops[lax.rem(c, SLOTS)] = rows[3:6]
        for kind in (S_UP, S_DOWN, S_UP2, S_DOWN2):
            start(kind, c)

    def mix(c):
        for kind in (S_UP, S_DOWN, S_UP2, S_DOWN2):
            await_recv(kind, c)
        mine = (st[c, 0, 0], st[c, 0, 1], st[c, 1, 0])
        near = (sb[c, 0, 1], sb[c, 0, 0], sb[c, 1, 1])
        far = (sb[c, 2, 0], sb[c, 1, 0], sb[c, 3, 0])
        mine, near, far = [jnp.concatenate(x, axis=0) for x in (mine, near, far)]
        top = jnp.maximum(mine, jnp.maximum(near, far))
        whole = top + jnp.log2(jnp.exp2(mine - top) + jnp.exp2(near - top) + jnp.exp2(far - top))
        rows = jnp.exp2(tops[lax.rem(c, SLOTS)] - whole)
        factor = jnp.concatenate([rows, jnp.zeros((HD - 3, HD), F32)], axis=0).T
        for g in range(GROUP):
            v9 = kv[c, :, :, 1, :, head(g)].reshape(keys, HD)
            weights = []
            for slot in range(3):
                p = pbuf[lax.rem(c, SLOTS), g, pl.ds(slot * tile, tile), :]
                weights.append((p * factor[g * tile:(g + 1) * tile, slot:slot + 1]).astype(BF16))
            o3 = jnp.dot(jnp.concatenate(weights, axis=0), v9, preferred_element_type=F32)
            oout[c, 0, :, head(g)] = o3[:tile].astype(BF16)
            oout[c, 1, :, head(g)] = o3[2 * tile:].astype(BF16)
            oacc[c, :, head(g)] = o3[tile:2 * tile]
        start(O_UP, c)
        start(O_DOWN, c)

    def store(c):
        columns = pl.ds(pl.multiple_of(c * width, HD), width)
        return pltpu.make_async_copy(out_vm.at[:, columns], out_hbm.at[:, columns], out_sem.at[c])

    def settle(c):
        await_send(O_UP, c)
        await_send(O_DOWN, c)
        store(c).wait()

    def finish(c):
        await_recv(O_UP, c)
        await_recv(O_DOWN, c)
        total = oacc[c] + oin[c, 0].astype(F32) + oin[c, 1].astype(F32)
        out_vm[:, pl.ds(pl.multiple_of(c * width, HD), width)] = total.astype(BF16)
        store(c).start()
        for kind in range(O_UP):
            await_send(kind, c)

        @pl.when(c >= 1)
        def _():
            settle(c - 1)


    def step(s, carry):
        for lag, stage in zip(LAGS, (relay, scores, mix, finish)):
            @pl.when((s >= lag) & (s < chunks + lag))
            def _():
                stage(s - lag)
        return carry

    lax.fori_loop(0, chunks + LAGS[-1], step, 0)

    settle(chunks - 1)
    for side in range(2):
        @pl.when((has_w_up, has_w_down)[side])
        def _():
            pen_copy(side).wait_send()


def body(sizes, query, keys, values, positions, window_reach):
    tile, width = query.shape[-2:]
    chunks = width // (GROUP * HD)
    wide = GROUP * HD
    flat = [x.reshape(tile, width) for x in (query, keys, values)]
    out = pl.pallas_call(
        functools.partial(kernel, sizes, chunks, tile),
        out_shape=jax.ShapeDtypeStruct((tile, width), BF16),
        in_specs=[pl.BlockSpec(memory_space=pltpu.HBM)] * 6,
        out_specs=pl.BlockSpec(memory_space=pltpu.HBM),
        scratch_shapes=[
            pltpu.VMEM(positions.shape, jnp.int32),
            pltpu.SMEM(window_reach.shape, jnp.int32),
            pltpu.VMEM((1, HD), F32),
            pltpu.VMEM((tile, width), BF16),
            pltpu.VMEM((tile, width), BF16),
            pltpu.VMEM((chunks, 3, 3, 2, tile, wide), BF16),
            pltpu.VMEM((chunks, 3, tile, wide), BF16),
            pltpu.VMEM((3, 8, HD), F32),
            pltpu.VMEM((3, 8, 5 * HD), F32),
            pltpu.VMEM((SLOTS, GROUP, 3 * tile, 9 * tile), F32),
            pltpu.VMEM((chunks, 2, 2, 1, HD), F32),
            pltpu.VMEM((chunks, 4, 2, 1, HD), F32),
            pltpu.VMEM((SLOTS, 3, HD), F32),
            pltpu.VMEM((chunks, 2, tile, wide), BF16),
            pltpu.VMEM((chunks, 2, tile, wide), BF16),
            pltpu.VMEM((chunks, tile, wide), F32),
            pltpu.VMEM((2, tile, HD), F32),
            pltpu.VMEM((HD, HD), BF16),
            pltpu.VMEM((tile, width), BF16),
            pltpu.SemaphoreType.DMA((chunks, KINDS)),
            pltpu.SemaphoreType.DMA((chunks, KINDS)),
            pltpu.SemaphoreType.DMA((2, 2)),
            pltpu.SemaphoreType.DMA((4,)),
            pltpu.SemaphoreType.DMA((chunks,)),
            pltpu.SemaphoreType.DMA((chunks,)),
            pltpu.SemaphoreType.DMA((chunks,)),
            pltpu.SemaphoreType.REGULAR((2,)),
        ],
        compiler_params=pltpu.CompilerParams(
            collective_id=0, has_side_effects=True, vmem_limit_bytes=54920 * 1024
        ),
        name="tile_attention",
    )(positions, window_reach, jnp.asarray(freq_row()), *flat)
    return out.reshape(query.shape)


def solution(mesh):
    in_specs = (
        P("ta", "ha", "wa", None, None),
        P("ta", "ha", "wa", None, None),
        P("ta", "ha", "wa", None, None),
        P(None, "ta", "ha", "wa", None),
        P("ta", "ha", "wa", None),
    )
    out_specs = P("ta", "ha", "wa", None, None)
    sizes = tuple(mesh.shape[a] for a in ("ta", "ha", "wa"))
    return jax.shard_map(
        functools.partial(body, sizes), mesh=mesh, in_specs=in_specs, out_specs=out_specs, check_vma=False
    )
```

```python
import functools
import math

import jax
import jax.numpy as jnp
import numpy as np
from jax import lax
from jax.experimental import pallas as pl
from jax.experimental.pallas import tpu as pltpu
from jax.sharding import PartitionSpec as P

HD = 128
RT = 16
RH = 56
RW = 56
GROUP = 2
AHEAD_K = 4
AHEAD_H = 4
AHEAD_Q = 2
LAGS = (0, 2, 5, 8)
SLOTS = LAGS[2] - LAGS[1] + 1
NEG = -1e30
SCALE2 = math.log2(math.e) / math.sqrt(HD)
F32 = jnp.float32
BF16 = jnp.bfloat16
MESH = pl.DeviceIdType.MESH

T_OUT, T_IN, HC_UP, HC_DOWN, HI_UP, HI_DOWN, HO_UP, HO_DOWN, Q_UP, Q_DOWN = range(10)
S_UP, S_DOWN, S_UP2, S_DOWN2, O_UP, O_DOWN = range(10, 16)
KINDS = 16


def freq_row():
    parts = []
    for size in (RT, RH, RW):
        pairs = size // 2
        local = np.arange(pairs, dtype=np.float32)
        parts.append(np.float32(256.0) ** (np.float32(-2.0) * local / np.float32(size)))
    return np.repeat(np.concatenate(parts), 2)[None, :].astype(np.float32)


def sin_cos(x):
    n = jnp.floor(x * F32(2.0 / math.pi) + F32(0.5))
    r = x - n * F32(1.5703125)
    r = r - n * F32(4.837512969970703125e-4)
    r = r - n * F32(7.549789954891882e-8)
    z = r * r
    s = ((F32(-1.9515295891e-4) * z + F32(8.3321608736e-3)) * z - F32(1.6666654611e-1)) * z * r + r
    c = (F32(2.443315711809948e-5) * z - F32(1.388731625493765e-3)) * z + F32(4.166664568298827e-2)
    c = c * z * z - F32(0.5) * z + F32(1.0)
    quadrant = n.astype(jnp.int32) & 3
    odd = (quadrant & 1) == 1
    sine = jnp.where(odd, c, s)
    cosine = jnp.where(odd, s, c)
    sine = jnp.where(quadrant >= 2, -sine, sine)
    cosine = jnp.where((quadrant == 1) | (quadrant == 2), -cosine, cosine)
    return sine, cosine


def kernel(
    sizes, chunks, tile,
    pos_hbm, reach_hbm, freq_hbm, q_hbm, k_hbm, v_hbm, out_hbm,
    pos_ref, reach_ref, freq_ref, q_ref, k_ref, kv, qb, pen, bias, pbuf, st, sb, tops, oout, oin, oacc, sincos, swap_ref, out_vm, send_sem, recv_sem, pen_sem, load_sem, k_sem, v_sem, out_sem, entry_sem,
):
    nt, nh, nw = sizes
    t, h, w = lax.axis_index("ta"), lax.axis_index("ha"), lax.axis_index("wa")
    width = GROUP * HD

    odd = lax.rem(t, 2)
    even = odd == 0
    i_out, i_in = 1 + odd, 2 - odd
    t_out, t_in = {"ta": t - 1 + 2 * odd}, {"ta": t + 1 - 2 * odd}
    h_up, h_down = {"ha": h + 1}, {"ha": h - 1}
    w_up, w_down, w_up2, w_down2 = {"wa": w + 1}, {"wa": w - 1}, {"wa": w + 2}, {"wa": w - 2}
    has_out = (t - 1 + 2 * odd >= 0) & (t - 1 + 2 * odd < nt)
    always = t >= 0
    has_h_up, has_h_down = h + 1 < nh, h >= 1
    has_w_up, has_w_down, has_w_up2, has_w_down2 = w + 1 < nw, w >= 1, w + 2 < nw, w >= 2
    beside = (
        (h_up, has_h_up), (h_down, has_h_down), (w_up, has_w_up), (w_down, has_w_down),
        (w_up2, has_w_up2), (w_down2, has_w_down2),
    )
    upward = {HC_UP, HI_UP, HO_UP, Q_UP, S_UP, S_UP2, O_UP}
    pairs = {
        HC_UP: (has_h_up, has_h_down), HI_UP: (has_h_up, has_h_down),
        HO_UP: (has_h_up & has_out, has_h_down & has_out),
        Q_UP: (has_w_up, has_w_down), S_UP: (has_w_up, has_w_down), O_UP: (has_w_up, has_w_down),
        S_UP2: (has_w_up2, has_w_down2),
    }

    barrier = pltpu.get_barrier_semaphore()

    @pl.when(has_out & (odd == 1))
    def _():
        pl.semaphore_signal(barrier, inc=1, device_id=t_out, device_id_type=MESH)

    for other, there in beside:
        @pl.when(there)
        def _():
            pl.semaphore_signal(barrier, inc=1, device_id={"ta": t + 1 - odd, **other}, device_id_type=MESH)

    @pl.when(even)
    def _():
        pl.semaphore_signal(barrier, inc=1, device_id=t_in, device_id_type=MESH)

    pos_load, freq_load, reach_load, q_load = [
        pltpu.make_async_copy(src, dst, load_sem.at[i])
        for i, (src, dst) in enumerate(
            ((pos_hbm, pos_ref), (freq_hbm, freq_ref), (reach_hbm, reach_ref), (q_hbm, q_ref))
        )
    ]

    def load_k(c):
        columns = pl.ds(pl.multiple_of(c * width, HD), width)
        return pltpu.make_async_copy(k_hbm.at[:, columns], k_ref.at[:, columns], k_sem.at[c])

    def load_v(c):
        columns = pl.ds(pl.multiple_of(c * width, HD), width)
        return pltpu.make_async_copy(v_hbm.at[:, columns], kv.at[c, 0, 0, 1], v_sem.at[c])

    pos_load.start()
    freq_load.start()
    for c in range(chunks):
        load_k(c).start()
        load_v(c).start()
    reach_load.start()
    q_load.start()

    def copy(kind, c, landing=False):
        own, outer, inner = kv.at[c, 0, 0], kv.at[c, 0, i_out], kv.at[c, 0, i_in]
        src, dst, to = {
            T_OUT: lambda: (own, outer if landing else inner, t_out),
            T_IN: lambda: (own, inner if landing else outer, t_in),
            HC_UP: lambda: (own, kv.at[c, 1, 0], h_up),
            HC_DOWN: lambda: (own, kv.at[c, 2, 0], h_down),
            HI_UP: lambda: (inner, kv.at[c, 1, i_in], h_up),
            HI_DOWN: lambda: (inner, kv.at[c, 2, i_in], h_down),
            HO_UP: lambda: (outer, kv.at[c, 1, i_out], h_up),
            HO_DOWN: lambda: (outer, kv.at[c, 2, i_out], h_down),
            Q_UP: lambda: (qb.at[c, 1], qb.at[c, 0], w_up),
            Q_DOWN: lambda: (qb.at[c, 1], qb.at[c, 2], w_down),
            S_UP: lambda: (st.at[c, 1], sb.at[c, 0], w_up),
            S_DOWN: lambda: (st.at[c, 0], sb.at[c, 1], w_down),
            S_UP2: lambda: (st.at[c, 1, 0], sb.at[c, 2, 0], w_up2),
            S_DOWN2: lambda: (st.at[c, 0, 0], sb.at[c, 3, 0], w_down2),
            O_UP: lambda: (oout.at[c, 1], oin.at[c, 0], w_up),
            O_DOWN: lambda: (oout.at[c, 0], oin.at[c, 1], w_down),
        }[kind]()
        return pltpu.make_async_remote_copy(
            src_ref=src, dst_ref=dst, send_sem=send_sem.at[c, kind], recv_sem=recv_sem.at[c, kind],
            device_id=to, device_id_type=MESH,
        )

    def guard(kind, receiving):
        if kind in (T_OUT, T_IN):
            return has_out if kind == T_OUT else always
        up, down = pairs[kind if kind in upward else kind - 1]
        return up if (kind in upward) != receiving else down

    def start(kind, c):
        @pl.when(guard(kind, False))
        def _():
            copy(kind, c).start()

    def await_recv(kind, c):
        @pl.when(guard(kind, True))
        def _():
            copy(kind, c, True).wait_recv()

    def await_send(kind, c):
        @pl.when(guard(kind, False))
        def _():
            copy(kind, c).wait_send()

    def blank(c, carry):
        def fill(missing, ref, index, value=0.0):
            @pl.when(missing)
            def _():
                ref[index] = jnp.full(ref.at[index].shape, value, ref.dtype)

        fill(jnp.logical_not(has_out), kv, (c, slice(None), i_out))
        fill(h < 1, kv, (c, 1))
        fill(h + 1 >= nh, kv, (c, 2))
        for side, (one, two) in enumerate(((w < 1, w < 2), (w + 1 >= nw, w + 2 >= nw))):
            fill(one, qb, (c, 2 * side))
            fill(one, oin, (c, side))
            fill(one, pen, 2 * side)
            fill(one, sb, (c, side), NEG)
            fill(two, sb, (c, 2 + side), NEG)
        return carry

    def pen_copy(side):
        return pltpu.make_async_remote_copy(
            src_ref=pen.at[1], dst_ref=pen.at[2 * side], send_sem=pen_sem.at[0, side],
            recv_sem=pen_sem.at[1, side], device_id=(w_up, w_down)[side], device_id_type=MESH,
        )

    a = lax.broadcasted_iota(jnp.int32, (HD, HD), 0)
    b = lax.broadcasted_iota(jnp.int32, (HD, HD), 1)
    swap = jnp.where((a ^ 1) == b, jnp.where((b & 1) == 1, F32(1.0), F32(-1.0)), F32(0.0))
    swap_ref[...] = swap.astype(BF16)
    pos_load.wait()
    freq_load.wait()
    dim = lax.broadcasted_iota(jnp.int32, (HD, tile), 0)
    place = [pos_ref[i, 0, 0, :, :].astype(F32) for i in range(3)]
    place = jnp.where(dim < RT, place[0], jnp.where(dim < RT + RH, place[1], place[2]))
    sine, cosine = sin_cos(place.T * freq_ref[...])
    sincos[0] = sine
    sincos[1] = cosine

    def rotated(ref, c, g):
        x = ref[:, pl.ds(pl.multiple_of(c * width + g * HD, HD), HD)]
        partner = jnp.dot(x, swap_ref[...], preferred_element_type=F32)
        return (x.astype(F32) * sincos[1] + partner * sincos[0]).astype(BF16)

    def head(g):
        return pl.ds(g * HD, HD)

    def turn_k(c):
        load_k(c).wait()
        for g in range(GROUP):
            kv[c, 0, 0, 0, :, head(g)] = rotated(k_ref, c, g)
        load_v(c).wait()

    def send_q(c):
        for g in range(GROUP):
            qb[c, 1, :, head(g)] = rotated(q_ref, c, g)
        start(Q_UP, c)
        start(Q_DOWN, c)

    turn_k(0)
    near_sem, far_sem = entry_sem.at[0], entry_sem.at[1]

    @pl.when(even & has_out)
    def _():
        pl.semaphore_wait(barrier, 1)
        pl.semaphore_signal(far_sem, inc=1, device_id=t_out, device_id_type=MESH)
        start(T_OUT, 0)

    for c in range(1, min(AHEAD_K, chunks)):
        turn_k(c)

        @pl.when(even & has_out)
        def _():
            start(T_OUT, c)

    @pl.when(odd == 1)
    def _():
        pl.semaphore_wait(barrier, 1 + 2 * sum(there.astype(jnp.int32) for _, there in beside))
        pl.semaphore_signal(near_sem, inc=1, device_id=t_in, device_id_type=MESH)

    @pl.when(even)
    def _():
        pl.semaphore_wait(near_sem, 1)

    lax.fori_loop(0, chunks, blank, 0)

    reach_load.wait()
    row = lax.broadcasted_iota(jnp.int32, (8, HD), 0)
    closed = jnp.zeros((8, HD), F32)
    for side, edge in enumerate(
        (t >= 1, t + 1 < nt, h >= 1, h + 1 < nh, w >= 1, w + 1 < nw)
    ):
        value = jnp.where((reach_ref[0, 0, 0, side] == 1) & edge, F32(0.0), F32(NEG))
        closed = jnp.where(row == side, value, closed)
    pen[1] = closed
    for side in range(2):
        @pl.when((has_w_up, has_w_down)[side])
        def _():
            pen_copy(side).start()
    q_load.wait()

    def send_own(c, carry):
        @pl.when(c >= AHEAD_K)
        def _():
            turn_k(c)

        start(T_IN, c)

        @pl.when(c < AHEAD_H)
        def _():
            start(HC_UP, c)
            start(HC_DOWN, c)

        @pl.when(c < AHEAD_Q)
        def _():
            send_q(c)

        return carry

    lax.fori_loop(0, chunks, send_own, 0)

    def relay_in(c, carry):
        await_recv(T_IN, c)

        @pl.when(c < AHEAD_H)
        def _():
            start(HI_UP, c)
            start(HI_DOWN, c)

        return carry

    lax.fori_loop(0, chunks, relay_in, 0)

    @pl.when((odd == 1) & has_out)
    def _():
        pl.semaphore_wait(far_sem, 1)
        for c in range(min(AHEAD_K, chunks)):
            start(T_OUT, c)

    def make_bias():
        for side in range(2):
            @pl.when((has_w_down, has_w_up)[side])
            def _():
                pen_copy(side).wait_recv()

        low = lax.broadcasted_iota(jnp.int32, (8, HD), 1) < tile
        for slot in range(3):
            rows = [jnp.broadcast_to(pen[slot, pl.ds(i, 1), :], (8, HD)) for i in range(6)]
            base = (rows[5], jnp.zeros((8, HD), F32), rows[4])[slot]
            along_t = (jnp.zeros((8, HD), F32), rows[0], rows[1])
            along_h = (jnp.zeros((8, HD), F32), rows[2], rows[3])
            tiles = [base + along_h[j] + along_t[i] for j in range(3) for i in range(3)]
            tiles.append(tiles[-1])
            for u in range(5):
                bias[slot, :, pl.ds(u * HD, HD)] = jnp.where(low, tiles[2 * u], tiles[2 * u + 1])

    keys = 9 * tile

    def relay(c):
        await_recv(T_OUT, c)
        start(HO_UP, c)
        start(HO_DOWN, c)

        @pl.when(c + AHEAD_K < chunks)
        def _():
            start(T_OUT, c + AHEAD_K)

        @pl.when(c + AHEAD_Q < chunks)
        def _():
            send_q(c + AHEAD_Q)

        @pl.when(c + AHEAD_H < chunks)
        def _():
            for kind in (HC_UP, HC_DOWN, HI_UP, HI_DOWN):
                start(kind, c + AHEAD_H)

    def scores(c):
        @pl.when(c == 0)
        def _():
            make_bias()

        for kind in (HC_UP, HC_DOWN, HI_UP, HI_DOWN, HO_UP, HO_DOWN, Q_UP, Q_DOWN):
            await_recv(kind, c)
        lane = lax.broadcasted_iota(jnp.int32, (tile, HD), 1)
        stats = []
        for g in range(GROUP):
            q3 = qb[c, :, :, head(g)].reshape(3 * tile, HD)
            k9 = kv[c, :, :, 0, :, head(g)].reshape(keys, HD)
            d3 = lax.dot_general(q3, k9, (((1,), (1,)), ((), ())), preferred_element_type=F32)
            columns = jnp.zeros((tile, HD), F32)
            for slot in range(3):
                d = d3[slot * tile:(slot + 1) * tile] + bias[slot, pl.ds(0, 1), pl.ds(0, keys)]
                m = jnp.max(d, axis=1, keepdims=True)
                p = jnp.exp2((d - m) * F32(SCALE2))
                total = jnp.sum(p, axis=1, keepdims=True)
                pbuf[lax.rem(c, SLOTS), g, pl.ds(slot * tile, tile), :] = p
                columns = jnp.where(lane == slot, m * F32(SCALE2) + jnp.log2(total), columns)
                columns = jnp.where(lane == 3 + slot, m * F32(SCALE2), columns)
            stats.append(columns)
        rows = jnp.concatenate(stats, axis=0).T
        st[c, 0, 0] = rows[0:1]
        st[c, 0, 1] = rows[1:2]
        st[c, 1, 0] = rows[2:3]
        st[c, 1, 1] = rows[1:2]
        tops[lax.rem(c, SLOTS)] = rows[3:6]
        for kind in (S_UP, S_DOWN, S_UP2, S_DOWN2):
            start(kind, c)

    def mix(c):
        for kind in (S_UP, S_DOWN, S_UP2, S_DOWN2):
            await_recv(kind, c)
        mine = (st[c, 0, 0], st[c, 0, 1], st[c, 1, 0])
        near = (sb[c, 0, 1], sb[c, 0, 0], sb[c, 1, 1])
        far = (sb[c, 2, 0], sb[c, 1, 0], sb[c, 3, 0])
        mine, near, far = [jnp.concatenate(x, axis=0) for x in (mine, near, far)]
        top = jnp.maximum(mine, jnp.maximum(near, far))
        whole = top + jnp.log2(jnp.exp2(mine - top) + jnp.exp2(near - top) + jnp.exp2(far - top))
        rows = jnp.exp2(tops[lax.rem(c, SLOTS)] - whole)
        factor = jnp.concatenate([rows, jnp.zeros((HD - 3, HD), F32)], axis=0).T
        for g in range(GROUP):
            v9 = kv[c, :, :, 1, :, head(g)].reshape(keys, HD)
            weights = []
            for slot in range(3):
                p = pbuf[lax.rem(c, SLOTS), g, pl.ds(slot * tile, tile), :]
                weights.append((p * factor[g * tile:(g + 1) * tile, slot:slot + 1]).astype(BF16))
            o3 = jnp.dot(jnp.concatenate(weights, axis=0), v9, preferred_element_type=F32)
            oout[c, 0, :, head(g)] = o3[:tile].astype(BF16)
            oout[c, 1, :, head(g)] = o3[2 * tile:].astype(BF16)
            oacc[c, :, head(g)] = o3[tile:2 * tile]
        start(O_UP, c)
        start(O_DOWN, c)

    def store(c):
        columns = pl.ds(pl.multiple_of(c * width, HD), width)
        return pltpu.make_async_copy(out_vm.at[:, columns], out_hbm.at[:, columns], out_sem.at[c])

    def settle(c):
        await_send(O_UP, c)
        await_send(O_DOWN, c)
        store(c).wait()

    def finish(c):
        await_recv(O_UP, c)
        await_recv(O_DOWN, c)
        total = oacc[c] + oin[c, 0].astype(F32) + oin[c, 1].astype(F32)
        out_vm[:, pl.ds(pl.multiple_of(c * width, HD), width)] = total.astype(BF16)
        store(c).start()
        for kind in range(O_UP):
            await_send(kind, c)

        @pl.when(c >= 1)
        def _():
            settle(c - 1)


    def step(s, carry):
        for lag, stage in zip(LAGS, (relay, scores, mix, finish)):
            @pl.when((s >= lag) & (s < chunks + lag))
            def _():
                stage(s - lag)
        return carry

    lax.fori_loop(0, chunks + LAGS[-1], step, 0)

    settle(chunks - 1)
    for side in range(2):
        @pl.when((has_w_up, has_w_down)[side])
        def _():
            pen_copy(side).wait_send()


def body(sizes, query, keys, values, positions, window_reach):
    tile, width = query.shape[-2:]
    chunks = width // (GROUP * HD)
    wide = GROUP * HD
    flat = [x.reshape(tile, width) for x in (query, keys, values)]
    out = pl.pallas_call(
        functools.partial(kernel, sizes, chunks, tile),
        out_shape=jax.ShapeDtypeStruct((tile, width), BF16),
        in_specs=[pl.BlockSpec(memory_space=pltpu.HBM)] * 6,
        out_specs=pl.BlockSpec(memory_space=pltpu.HBM),
        scratch_shapes=[
            pltpu.VMEM(positions.shape, jnp.int32),
            pltpu.SMEM(window_reach.shape, jnp.int32),
            pltpu.VMEM((1, HD), F32),
            pltpu.VMEM((tile, width), BF16),
            pltpu.VMEM((tile, width), BF16),
            pltpu.VMEM((chunks, 3, 3, 2, tile, wide), BF16),
            pltpu.VMEM((chunks, 3, tile, wide), BF16),
            pltpu.VMEM((3, 8, HD), F32),
            pltpu.VMEM((3, 8, 5 * HD), F32),
            pltpu.VMEM((SLOTS, GROUP, 3 * tile, 9 * tile), F32),
            pltpu.VMEM((chunks, 2, 2, 1, HD), F32),
            pltpu.VMEM((chunks, 4, 2, 1, HD), F32),
            pltpu.VMEM((SLOTS, 3, HD), F32),
            pltpu.VMEM((chunks, 2, tile, wide), BF16),
            pltpu.VMEM((chunks, 2, tile, wide), BF16),
            pltpu.VMEM((chunks, tile, wide), F32),
            pltpu.VMEM((2, tile, HD), F32),
            pltpu.VMEM((HD, HD), BF16),
            pltpu.VMEM((tile, width), BF16),
            pltpu.SemaphoreType.DMA((chunks, KINDS)),
            pltpu.SemaphoreType.DMA((chunks, KINDS)),
            pltpu.SemaphoreType.DMA((2, 2)),
            pltpu.SemaphoreType.DMA((4,)),
            pltpu.SemaphoreType.DMA((chunks,)),
            pltpu.SemaphoreType.DMA((chunks,)),
            pltpu.SemaphoreType.DMA((chunks,)),
            pltpu.SemaphoreType.REGULAR((2,)),
        ],
        compiler_params=pltpu.CompilerParams(
            collective_id=0, has_side_effects=True, vmem_limit_bytes=54920 * 1024
        ),
        name="tile_attention",
    )(positions, window_reach, jnp.asarray(freq_row()), *flat)
    return out.reshape(query.shape)


def solution(mesh):
    in_specs = (
        P("ta", "ha", "wa", None, None),
        P("ta", "ha", "wa", None, None),
        P("ta", "ha", "wa", None, None),
        P(None, "ta", "ha", "wa", None),
        P("ta", "ha", "wa", None),
    )
    out_specs = P("ta", "ha", "wa", None, None)
    sizes = tuple(mesh.shape[a] for a in ("ta", "ha", "wa"))
    return jax.shard_map(
        functools.partial(body, sizes), mesh=mesh, in_specs=in_specs, out_specs=out_specs, check_vma=False
    )
```
